32 devices in a mesh: feat: 8 (over z, y), dp: 4 (over x, core).
Axes of the slice: x: 2, y: 2, z: 4, core: 2. Of those that a mesh axis runs over, the one named last changes fastest.
Arguments:
- face_grid: bfloat16 [4096, 10240], P('dp', 'feat'), may hold values from -6 to 6
- first_nbrs: int32 [2048, 8], P('dp'), may hold values from 0 to 1023
- first_count: int32 [2048], P('dp'), may hold values from 1 to 8
- w_first: bfloat16 [10240, 256], P('feat'), may hold values from -0.0625 to 0.0625
- b_first: float32 [256], replicated, may hold values from -3 to 3
- send_rows: int32 [512], P('dp'), may hold values from 0 to 511
- second_nbrs: int32 [2048, 8], P(('dp', 'feat')), may hold values from 0 to 639
- second_count: int32 [2048], P(('dp', 'feat')), may hold values from 1 to 8
- w_in: bfloat16 [256, 1024], replicated, may hold values from -0.375 to 0.375
- w_out: bfloat16 [1024, 256], replicated, may hold values from -0.1875 to 0.1875
- out_grad: bfloat16 [2048, 256], P(('dp', 'feat')), may hold values from -6 to 6
Outputs:
- embed: bfloat16 [2048, 256], P(('dp', 'feat'))
- grad_first: float32 [10240, 256], P('feat')
The draws below stay inside these ranges and needn't reach their ends.
Inputs may be any that keep to these rules, and one draw needn't show every extreme that they name: `first_count`: slots at or past a target's count are ignored; counts lie in 1 to 8. `first_nbrs`: only slots below first_count are read. `second_count`: slots at or past a target's count are ignored. `second_nbrs`: indices below 512 name the partition's own targets, the rest the faces received from the previous partition in order; only slots below second_count are read. `send_rows`: entries may repeat.
All inputs are finite; a program needn't handle non-finite values.
Results may differ from the reference program's by a relative error of at most 0.0061.
Values may be sent and summed in bfloat16 or wider, within the bound.
A program may use at most 64 MiB of HBM per device.

```python
import jax
import jax.numpy as jnp
from jax import lax

F = 10240
HID = 256
MLP = 1024
K = 8
G = 512
SRC = 1024
HALO = 128
N_DP = 4


def plant(values, rng, least, largest):
    spot = [jax.random.randint(jax.random.fold_in(rng, axis), (), 0, length) for axis, length in enumerate(values.shape)]
    widest = values.shape.index(max(values.shape))
    neighbour = spot[:widest] + [(spot[widest] + 1) % values.shape[widest]] + spot[widest + 1:]
    return values.at[tuple(spot)].set(least).at[tuple(neighbour)].set(largest)


def block_levels(own_key, extent, pieces, smallest, high):
    gain, own = 1.0, jax.random.fold_in(own_key, 6)
    for position, blocks in pieces:
        draws = jnp.exp(jax.random.uniform(jax.random.fold_in(own, position), (blocks,), jnp.float32, smallest / len(pieces), high / len(pieces)))
        gain = gain * jnp.repeat(draws, extent[position] // blocks).reshape([-1 if axis == position else 1 for axis in range(len(extent))])
    return gain


def gaussian(stream_key, extent, scale, limit, cuts=(), kind=jnp.bfloat16):
    array = scale * jax.random.normal(stream_key, extent, jnp.float32)
    if cuts:
        array = array * block_levels(stream_key, extent, cuts, -0.22, 0.18)
    return jnp.clip(array, -limit, limit).astype(kind)


def setup_inputs(seed: int = 0) -> dict:
    seeds = jax.random.split(jax.random.key(seed), 12)
    return {
        "face_grid": gaussian(seeds[0], (N_DP * SRC, F), 1.0, 6.0, ((0, 4), (1, 8))),
        "first_nbrs": plant(jax.random.randint(seeds[1], (N_DP * G, K), 0, SRC), jax.random.fold_in(seeds[1], 1), 0, SRC - 1).astype(jnp.int32),
        "first_count": plant(jax.random.randint(seeds[2], (N_DP * G,), 1, K + 1), jax.random.fold_in(seeds[2], 1), 1, K).astype(jnp.int32),
        "w_first": gaussian(seeds[3], (F, HID), F ** -0.5, 0.0625, ((0, 8),)),
        "b_first": gaussian(seeds[4], (HID,), 0.5, 3.0, (), jnp.float32),
        "send_rows": plant(jax.random.randint(seeds[5], (N_DP * HALO,), 0, G), jax.random.fold_in(seeds[5], 1), 0, G - 1).astype(jnp.int32),
        "second_nbrs": plant(jax.random.randint(seeds[6], (N_DP * G, K), 0, G + HALO), jax.random.fold_in(seeds[6], 1), 0, (G + HALO) - 1).astype(jnp.int32),
        "second_count": plant(jax.random.randint(seeds[7], (N_DP * G,), 1, K + 1), jax.random.fold_in(seeds[7], 1), 1, K).astype(jnp.int32),
        "w_in": gaussian(seeds[8], (HID, MLP), HID ** -0.5, 0.375),
        "w_out": gaussian(seeds[9], (MLP, HID), MLP ** -0.5, 0.1875),
        "out_grad": gaussian(seeds[10], (N_DP * G, HID), 1.0, 6.0, ((0, 32),)),
    }


def slope(value):
    sig = jax.nn.sigmoid(value)
    return sig * (1.0 + value * (1.0 - sig))


def mean_rows(table, nbrs, count):
    total = jnp.zeros((nbrs.shape[0], table.shape[1]), jnp.float32)
    for slot in range(nbrs.shape[1]):
        picked = table[nbrs[:, slot]].astype(jnp.float32)
        total = total + jnp.where((slot < count)[:, None], picked, 0.0)
    return total / count[:, None].astype(jnp.float32)


def spread(grad, nbrs, count, size):
    slots = jnp.arange(nbrs.shape[1], dtype=jnp.int32)
    factor = jnp.where(slots[None, :] < count[:, None], 1.0 / count[:, None].astype(jnp.float32), 0.0)
    terms = (grad[:, None, :] * factor[:, :, None]).reshape(-1, grad.shape[1])
    return jax.ops.segment_sum(terms, nbrs.reshape(-1), num_segments=size)


def reference(face_grid, first_nbrs, first_count, w_first, b_first, send_rows, second_nbrs, second_count, w_in, w_out, out_grad):
    agg_list, pre_list, hid_list = [], [], []
    for part in range(N_DP):
        sources = face_grid[part * SRC:(part + 1) * SRC]
        nbrs = first_nbrs[part * G:(part + 1) * G]
        count = first_count[part * G:(part + 1) * G]
        agg = (sources[:G].astype(jnp.float32) + mean_rows(sources, nbrs, count)).astype(jnp.bfloat16)
        pre = jnp.dot(agg, w_first, preferred_element_type=jnp.float32) + b_first
        agg_list.append(agg)
        pre_list.append(pre)
        hid_list.append(jax.nn.silu(pre).astype(jnp.bfloat16))
    embeds, grad_aggs, grad_exts = [], [], []
    for part in range(N_DP):
        prev = (part - 1) % N_DP
        sent = hid_list[prev][send_rows[prev * HALO:(prev + 1) * HALO]]
        extended = jnp.concatenate([hid_list[part], sent], axis=0)
        nbrs = second_nbrs[part * G:(part + 1) * G]
        count = second_count[part * G:(part + 1) * G]
        agg2 = (hid_list[part].astype(jnp.float32) + mean_rows(extended, nbrs, count)).astype(jnp.bfloat16)
        pre_mlp = jnp.dot(agg2, w_in, preferred_element_type=jnp.float32)
        act = jax.nn.silu(pre_mlp).astype(jnp.bfloat16)
        embeds.append((hid_list[part].astype(jnp.float32) + jnp.dot(act, w_out, preferred_element_type=jnp.float32)).astype(jnp.bfloat16))
        cot = out_grad[part * G:(part + 1) * G]
        grad_act = lax.dot_general(cot, w_out, (((1,), (1,)), ((), ())), preferred_element_type=jnp.float32)
        grad_pre = (grad_act * slope(pre_mlp)).astype(jnp.bfloat16)
        grad_agg = lax.dot_general(grad_pre, w_in, (((1,), (1,)), ((), ())), preferred_element_type=jnp.float32)
        grad_aggs.append(grad_agg)
        grad_exts.append(spread(grad_agg, nbrs, count, G + HALO))
    grad_first = jnp.zeros((F, HID), jnp.float32)
    for part in range(N_DP):
        nxt = (part + 1) % N_DP
        cot = out_grad[part * G:(part + 1) * G].astype(jnp.float32)
        table_grad = grad_exts[part][:G].at[send_rows[part * HALO:(part + 1) * HALO]].add(grad_exts[nxt][G:])
        grad_hidden = cot + grad_aggs[part] + table_grad
        grad_pre = (grad_hidden * slope(pre_list[part])).astype(jnp.bfloat16)
        grad_first = grad_first + lax.dot_general(agg_list[part], grad_pre, (((0,), (0,)), ((), ())), preferred_element_type=jnp.float32)
    return jnp.concatenate(embeds, axis=0), grad_first
```

```python
import functools

import jax
import jax.numpy as jnp
from jax import lax
from jax.experimental import pallas as pl
from jax.experimental.pallas import tpu as pltpu
from jax.sharding import PartitionSpec as P

MESH = pl.DeviceIdType.MESH
F32, BF16 = jnp.float32, jnp.bfloat16


def dot(a, b):
    return jnp.dot(a, b, preferred_element_type=F32)


def dot_first(a, b):
    return lax.dot_general(a, b, (((0,), (0,)), ((), ())), preferred_element_type=F32)


def dot_last(a, b):
    return lax.dot_general(a, b, (((1,), (1,)), ((), ())), preferred_element_type=F32)


def slope(value):
    sig = jax.nn.sigmoid(value)
    return sig * (1.0 + value * (1.0 - sig))


def steps(count, fn):
    if count <= 2:
        for i in range(count):
            fn(i)
    else:
        pl.loop(0, count)(fn)


def split(size, width):
    return [(at, min(width, size - at)) for at in range(0, size, width)]


def counts_matrix(nbrs, source, out, at, rows, width):
    def group(g):
        names = nbrs[pl.ds(pl.multiple_of(source + g * 16, 16), 16), :8]
        for lane, size in split(width, 1024):
            spot = lax.broadcasted_iota(jnp.int32, (16, size), 1).astype(names.dtype) + lane
            total = jnp.zeros((16, size), F32)
            for slot in range(8):
                total = total + jnp.where(names[:, slot : slot + 1] == spot, 1.0, 0.0)
            out[pl.ds(pl.multiple_of(at + g * 16, 16), 16), lane : lane + size] = total.astype(BF16)

    pl.loop(0, rows // 16)(group)


def inverse(names):
    live = jnp.where(names >= 0, 1.0, 0.0)
    return 1.0 / jnp.sum(live, axis=1, keepdims=True)


def kernel(
    n, parts, block, chunks,
    face_hbm, nb1, w1_hbm, b1, srows, nb2, win_hbm, wout_hbm, og,
    embed, grad,
    face, w1, win, wout, adj, agg, agg_t, part32, part16, rs_buf, pre_own, pre_all,
    ext, picks, og_all, nb_pad, nb_send, nb_all, nb_nat, smat, grad_act, agg2, gscaled, gagg,
    halo_out, back_out, back_in, gtotal, gp, pair_out, pair_in, chip_buf,
    load_sem, rs_s, rs_r, ag_s, ag_r, og_s, og_r, nb_s, nb_r, halo_sem, back_sem,
    pa_s, pa_r, x_s, x_r, pb_s, pb_r,
):
    f, d = lax.axis_index("feat"), lax.axis_index("dp")
    src, width = face.shape
    targets, hid = nb1.shape[0], w1.shape[1]
    own = nb2.shape[0]
    halo = srows.shape[1]
    full = targets + halo
    mine = pl.ds(pl.multiple_of(f * own, own), own)
    cols = split(width, 256)

    loads = [
        pltpu.make_async_copy(face_hbm.at[:, pl.ds(at, size)], face.at[:, pl.ds(at, size)], load_sem.at[i])
        for i, (at, size) in enumerate(cols)
    ]
    loads.append(pltpu.make_async_copy(w1_hbm, w1, load_sem.at[len(cols)]))
    late = [
        pltpu.make_async_copy(wout_hbm, wout, load_sem.at[len(cols) + 1]),
        pltpu.make_async_copy(win_hbm, win, load_sem.at[len(cols) + 2]),
    ]
    for copy in loads + late:
        copy.start()

    barrier = pltpu.get_barrier_semaphore()
    for i in range(1, n):
        pl.semaphore_signal(barrier, inc=1, device_id={"feat": lax.rem(f + i, n)}, device_id_type=MESH)
    for i in range(1, parts):
        pl.semaphore_signal(barrier, inc=1, device_id={"dp": lax.rem(d + i, parts)}, device_id_type=MESH)

    nb_pad[...] = jnp.full(nb_pad.shape, -1.0, F32)
    nb_pad[:own, :8] = nb2[...].astype(F32)
    nb_send[...] = jnp.transpose(nb_pad[...])[:8]
    if nb_all.shape[0] > n * 8:
        nb_all[n * 8 :, :] = jnp.full((nb_all.shape[0] - n * 8, 128), -1.0, F32)
    nb_all[pl.ds(pl.multiple_of(f * 8, 8), 8), :] = nb_send[...]
    og_all[mine, :] = og[...]
    picks[...] = jnp.where(
        lax.broadcasted_iota(jnp.int32, (targets, halo), 0) == srows[...], 1.0, 0.0
    ).astype(BF16)

    pl.semaphore_wait(barrier, n - 1 + parts - 1)

    def gathered(source, buffer, rows, sends, recvs):
        place = buffer.at[pl.ds(pl.multiple_of(f * rows, rows), rows)]
        copies = []
        for i in range(1, n):
            copies.append(
                pltpu.make_async_remote_copy(
                    source, place, sends.at[i], recvs.at[i],
                    device_id={"feat": lax.rem(f + i, n)}, device_id_type=MESH,
                )
            )
        for copy in copies:
            copy.start()
        return copies

    nb_copies = gathered(nb_send, nb_all, 8, nb_s, nb_r)
    og_copies = gathered(og, og_all, own, og_s, og_r)

    blocks = targets // block
    per = block // own
    first = lax.rem(f // per + 1, blocks)

    def send_to(dest):
        return pltpu.make_async_remote_copy(
            part16.at[pl.ds(pl.multiple_of(dest * own, own), own)], rs_buf.at[f],
            rs_s.at[dest], rs_r.at[f], device_id={"feat": dest}, device_id_type=MESH,
        )

    if blocks > 2:
        for copy in loads:
            copy.wait()

    def first_layer(i):
        at = pl.multiple_of(lax.rem(first + i, blocks) * block, block)
        rows = pl.ds(at, block)
        counts_matrix(nb1, at, adj, 0, block, src)
        inv = inverse(nb1[rows, :])
        total = jnp.zeros((block, hid), F32)
        for j, (lane, size) in enumerate(cols):
            if blocks <= 2 and i == 0:
                loads[j].wait()
                if j == 0:
                    loads[-1].wait()
            chunk = slice(lane, lane + size)
            value = dot(adj[...], face[:, chunk]) * inv + face[rows, chunk].astype(F32)
            value = value.astype(BF16)
            agg[rows, chunk] = value
            total = total + dot(value, w1[chunk, :])
        part32[rows, :] = total
        part16[rows, :] = total.astype(BF16)
        for j in range(per):
            dest = lax.rem(first + i, blocks) * per + j
            pl.when(dest != f)(lambda dest=dest: send_to(dest).start())

    steps(blocks, first_layer)

    for lane, size in cols:
        agg_t[lane : lane + size, :] = jnp.transpose(agg[:, lane : lane + size])
    for copy in nb_copies:
        copy.wait()
    for at in range(0, nb_all.shape[0], 128):
        turned = jnp.transpose(nb_all[at : at + 128, :])
        for j in range(min(16, n - at // 8)):
            t = at // 8 + j
            nb_nat[t * own : (t + 1) * own, :8] = turned[:own, j * 8 : j * 8 + 8]
    counts_matrix(nb_nat, 0, smat, 0, targets, full)
    for copy in late + og_copies:
        copy.wait()

    def out_part(i):
        rows = pl.ds(pl.multiple_of(i * block, block), block)
        grad_act[rows, :] = dot_last(og_all[rows, :], wout[...])

    steps(blocks, out_part)

    value = part32[mine, :] + b1[...]
    for i in range(1, n):
        source = lax.rem(f + i, n)
        pltpu.make_async_remote_copy(
            part16.at[pl.ds(0, own)], rs_buf.at[source], rs_s.at[source], rs_r.at[source],
            device_id={"feat": source}, device_id_type=MESH,
        ).wait_recv()
        value = value + rs_buf[source].astype(F32)
    pre_own[...] = value.astype(BF16)
    pre_all[mine, :] = value.astype(BF16)
    for copy in gathered(pre_own, pre_all, own, ag_s, ag_r):
        copy.wait()

    ext[:targets, :] = jax.nn.silu(pre_all[...].astype(F32)).astype(BF16)
    halo_out[...] = dot_first(picks[...], ext[:targets, :]).astype(BF16)
    halo_copy = pltpu.make_async_remote_copy(
        halo_out, ext.at[pl.ds(targets, halo)], halo_sem.at[0], halo_sem.at[1],
        device_id={"dp": lax.rem(d + 1, parts)}, device_id_type=MESH,
    )
    halo_copy.start()

    def neighbour_part(i):
        rows = pl.ds(pl.multiple_of(i * block, block), block)
        gagg[rows, :] = dot(smat[rows, :targets], ext[:targets, :])

    steps(blocks, neighbour_part)
    halo_copy.wait()

    def second_layer(i):
        rows = pl.ds(pl.multiple_of(i * block, block), block)
        inv = inverse(nb_nat[rows, :8])
        total = gagg[rows, :] + dot(smat[rows, targets:], ext[targets:, :])
        value = (ext[rows, :].astype(F32) + total * inv).astype(BF16)
        agg2[rows, :] = value
        step = (grad_act[rows, :] * slope(dot(value, win[...]))).astype(BF16)
        back = dot_last(step, win[...])
        gagg[rows, :] = back
        gscaled[rows, :] = (back * inv).astype(BF16)

    steps(blocks, second_layer)

    back_out[...] = dot_first(smat[:, targets:], gscaled[...]).astype(BF16)
    back_copy = pltpu.make_async_remote_copy(
        back_out, back_in, back_sem.at[0], back_sem.at[1],
        device_id={"dp": lax.rem(d + parts - 1, parts)}, device_id_type=MESH,
    )
    back_copy.start()

    for at, size in split(targets, 512):
        rows = slice(at, at + size)
        gtotal[rows, :] = (
            og_all[rows, :].astype(F32) + gagg[rows, :] + dot_first(smat[:, rows], gscaled[...])
        )
    act = jax.nn.silu(dot(agg2[mine, :], win[...])).astype(BF16)
    embed[...] = (ext[mine, :].astype(F32) + dot(act, wout[...])).astype(BF16)

    back_copy.wait()
    gp[...] = (
        (gtotal[...] + dot(picks[...], back_in[...])) * slope(pre_all[...].astype(F32))
    ).astype(BF16)

    half = width // 2
    size = half // chunks
    side = lax.rem(d, 2)
    chip = d // 2
    chips = parts // 2
    mate = d + 1 - 2 * side

    def place(which, c):
        return pl.ds(pl.multiple_of(which * half + c * size, 16), size)

    pair_copies, chip_copies, end_copies = [], [], []
    for c in range(chunks):
        span = slice(c * size, (c + 1) * size)
        pair_out[span, :] = dot(agg_t[place(1 - side, c), :], gp[...]).astype(BF16)
        copy = pltpu.make_async_remote_copy(
            pair_out.at[pl.ds(c * size, size)], pair_in.at[pl.ds(c * size, size)], pa_s.at[c], pa_r.at[c],
            device_id={"dp": mate}, device_id_type=MESH,
        )
        copy.start()
        pair_copies.append(copy)
    for c in range(chunks):
        span = slice(c * size, (c + 1) * size)
        value = dot(agg_t[place(side, c), :], gp[...])
        pair_copies[c].wait()
        chip_buf[chip, span, :] = (value + pair_in[span, :].astype(F32)).astype(BF16)
        for i in range(1, chips):
            here = chip_buf.at[chip, pl.ds(c * size, size)]
            copy = pltpu.make_async_remote_copy(
                here, here, x_s.at[i, c], x_r.at[i, c],
                device_id={"dp": lax.rem(d + 2 * i, parts)}, device_id_type=MESH,
            )
            copy.start()
            chip_copies.append(copy)
    for c in range(chunks):
        span = slice(c * size, (c + 1) * size)
        for copy in chip_copies[c * (chips - 1) : (c + 1) * (chips - 1)]:
            copy.wait()
        total = chip_buf[0, span, :].astype(F32)
        for i in range(1, chips):
            total = total + chip_buf[i, span, :].astype(F32)
        grad[place(side, c), :] = total.astype(BF16)
        there = grad.at[place(side, c)]
        copy = pltpu.make_async_remote_copy(
            there, there, pb_s.at[c], pb_r.at[c], device_id={"dp": mate}, device_id_type=MESH,
        )
        copy.start()
        end_copies.append(copy)
    for copy in end_copies:
        copy.wait()
    for i in range(1, n):
        send_to(lax.rem(f + i, n)).wait_send()


def fused(n, parts, face_grid, nb1, w_first, b_first, send_rows, nb2, w_in, w_out, out_grad):
    src, width = face_grid.shape
    targets, hid = nb1.shape[0], w_first.shape[1]
    inner = w_in.shape[1]
    own, halo = nb2.shape[0], send_rows.shape[1]
    full = targets + halo
    block = min(targets, 256)
    half = width // 2
    chunks = next(c for c in (4, 2, 1) if (half // c) % 16 == 0)
    chips = parts // 2
    tiles = -(-n * 8 // 128) * 128
    any_space = pl.BlockSpec(memory_space=pl.ANY)
    vmem = pl.BlockSpec(memory_space=pltpu.VMEM)
    dma = pltpu.SemaphoreType.DMA
    return pl.pallas_call(
        functools.partial(kernel, n, parts, block, chunks),
        out_shape=(
            jax.ShapeDtypeStruct((own, hid), BF16),
            jax.ShapeDtypeStruct((width, hid), BF16),
        ),
        in_specs=[any_space, vmem, any_space, vmem, vmem, vmem, any_space, any_space, vmem],
        out_specs=(vmem, vmem),
        scratch_shapes=[
            pltpu.VMEM((src, width), BF16),
            pltpu.VMEM((width, hid), BF16),
            pltpu.VMEM((hid, inner), BF16),
            pltpu.VMEM((inner, hid), BF16),
            pltpu.VMEM((block, src), BF16),
            pltpu.VMEM((targets, width), BF16),
            pltpu.VMEM((width, targets), BF16),
            pltpu.VMEM((targets, hid), F32),
            pltpu.VMEM((targets, hid), BF16),
            pltpu.VMEM((n, own, hid), BF16),
            pltpu.VMEM((own, hid), BF16),
            pltpu.VMEM((targets, hid), BF16),
            pltpu.VMEM((full, hid), BF16),
            pltpu.VMEM((targets, halo), BF16),
            pltpu.VMEM((targets, hid), BF16),
            pltpu.VMEM((128, 128), F32),
            pltpu.VMEM((8, 128), F32),
            pltpu.VMEM((tiles, 128), F32),
            pltpu.VMEM((targets, 128), F32),
            pltpu.VMEM((targets, full), BF16),
            pltpu.VMEM((targets, inner), F32),
            pltpu.VMEM((targets, hid), BF16),
            pltpu.VMEM((targets, hid), BF16),
            pltpu.VMEM((targets, hid), F32),
            pltpu.VMEM((halo, hid), BF16),
            pltpu.VMEM((halo, hid), BF16),
            pltpu.VMEM((halo, hid), BF16),
            pltpu.VMEM((targets, hid), F32),
            pltpu.VMEM((targets, hid), BF16),
            pltpu.VMEM((half, hid), BF16),
            pltpu.VMEM((half, hid), BF16),
            pltpu.VMEM((chips, half, hid), BF16),
            dma((len(split(width, 256)) + 3,)),
            dma((n,)), dma((n,)), dma((n,)), dma((n,)), dma((n,)), dma((n,)), dma((n,)), dma((n,)),
            dma((2,)), dma((2,)),
            dma((chunks,)), dma((chunks,)),
            dma((chips, chunks)), dma((chips, chunks)),
            dma((chunks,)), dma((chunks,)),
        ],
        compiler_params=pltpu.CompilerParams(
            collective_id=0, has_side_effects=True, vmem_limit_bytes=56 * 1024 * 1024
        ),
        cost_estimate=pl.CostEstimate(
            flops=2 * targets * src * width, bytes_accessed=2 * src * width, transcendentals=0
        ),
        name="fused_step",
    )(face_grid, nb1, w_first, b_first, send_rows, nb2, w_in, w_out, out_grad)


def live(nbrs, count):
    slots = jnp.arange(nbrs.shape[1], dtype=jnp.int32)
    return jnp.where(slots[None, :] < count[:, None], nbrs, -1)


def solution(mesh):
    n, parts = mesh.shape["feat"], mesh.shape["dp"]

    def body(
        face_grid, first_nbrs, first_count, w_first, b_first, send_rows,
        second_nbrs, second_count, w_in, w_out, out_grad,
    ):
        embed, grad = fused(
            n, parts, face_grid, live(first_nbrs, first_count), w_first, b_first.reshape(1, -1),
            send_rows.reshape(1, -1), live(second_nbrs, second_count), w_in, w_out, out_grad,
        )
        return embed, grad.astype(F32)

    return jax.shard_map(
        body,
        mesh=mesh,
        in_specs=(
            P("dp", "feat"), P("dp", None), P("dp"), P("feat", None), P(), P("dp"),
            P(("dp", "feat"), None), P(("dp", "feat")), P(), P(), P(("dp", "feat"), None),
        ),
        out_specs=(P(("dp", "feat"), None), P("feat", None)),
        check_vma=False,
    )
```

```python
import functools

import jax
import jax.numpy as jnp
from jax import lax
from jax.experimental import pallas as pl
from jax.experimental.pallas import tpu as pltpu
from jax.sharding import PartitionSpec as P

MESH = pl.DeviceIdType.MESH
F32, BF16 = jnp.float32, jnp.bfloat16


def dot(a, b):
    return jnp.dot(a, b, preferred_element_type=F32)


def dot_last(a, b):
    return lax.dot_general(a, b, (((1,), (1,)), ((), ())), preferred_element_type=F32)


def sigmoid(value):
    return 0.5 * jnp.tanh(0.5 * value) + 0.5


def slope(value):
    sig = sigmoid(value)
    return sig * (1.0 + value * (1.0 - sig))


def steps(count, fn):
    if count <= 2:
        for i in range(count):
            fn(i)
    else:
        pl.loop(0, count)(fn)


def split(size, width):
    return [(at, min(width, size - at)) for at in range(0, size, width)]


def counts_matrix(nbrs, source, out, at, rows, width):
    spots = [
        (lane, size, (lax.broadcasted_iota(jnp.int32, (8, size), 1) + lane).astype(F32))
        for lane, size in split(width, 1024)
    ]

    def group(g):
        for lane, size, spot in spots:
            pieces = []
            for piece in range(2):
                names = nbrs[pl.ds(pl.multiple_of(source + g * 16 + piece * 8, 8), 8), :8]
                total = jnp.zeros((8, size), F32)
                for slot in range(8):
                    total = total + jnp.where(names[:, slot : slot + 1] == spot, 1.0, 0.0)
                pieces.append(total)
            here = pl.ds(pl.multiple_of(at + g * 16, 16), 16)
            out[here, lane : lane + size] = jnp.concatenate(pieces, axis=0).astype(BF16)

    pl.loop(0, rows // 16)(group)


def live(nbrs, count):
    slots = lax.broadcasted_iota(jnp.int32, nbrs.shape, 0)
    return jnp.where(slots < count, nbrs, -1).astype(F32)


def inverse(names):
    live = jnp.where(names >= 0, 1.0, 0.0)
    return 1.0 / jnp.sum(live, axis=1, keepdims=True)


def kernel(
    n, parts, block, chunks,
    face_hbm, nb1_t, count1, w1_hbm, b1, srows, nb2_t, count2, win_hbm, wout_hbm, og,
    embed, grad,
    face, w1, win, wout, adj, agg, agg_t, part32, part16, rs_buf, pre_own, pre_all,
    ext, picks, picks_t, og_all, nb1, nb_send, nb_all, nb_nat, smat, smat_t, grad_act, agg2, gscaled, gagg,
    halo_out, back_out, back_in, gtotal, gp, pair_out, pair_in, chip_buf,
    load_sem, rs_s, rs_r, ag_s, ag_r, og_s, og_r, nb_s, nb_r, halo_sem, back_sem,
    pa_s, pa_r, x_s, x_r, pb_s, pb_r,
):
    f, d = lax.axis_index("feat"), lax.axis_index("dp")
    src, width = face.shape
    targets, hid = nb1.shape[0], w1.shape[1]
    own = og.shape[0]
    halo = srows.shape[1]
    full = targets + halo
    mine = pl.ds(pl.multiple_of(f * own, own), own)
    cols = split(width, 256)

    loads = [
        pltpu.make_async_copy(face_hbm.at[:, pl.ds(at, size)], face.at[:, pl.ds(at, size)], load_sem.at[i])
        for i, (at, size) in enumerate(cols)
    ]
    loads.append(pltpu.make_async_copy(w1_hbm, w1, load_sem.at[len(cols)]))
    late = [
        pltpu.make_async_copy(wout_hbm, wout, load_sem.at[len(cols) + 1]),
        pltpu.make_async_copy(win_hbm, win, load_sem.at[len(cols) + 2]),
    ]
    for copy in loads + late:
        copy.start()

    barrier = pltpu.get_barrier_semaphore()
    for i in range(1, n):
        pl.semaphore_signal(barrier, inc=1, device_id={"feat": lax.rem(f + i, n)}, device_id_type=MESH)
    for i in range(1, parts):
        pl.semaphore_signal(barrier, inc=1, device_id={"dp": lax.rem(d + i, parts)}, device_id_type=MESH)

    nb_send[...] = jnp.full(nb_send.shape, -1.0, F32)
    nb_send[:, :own] = live(nb2_t[...], count2[...])
    if nb_all.shape[0] > n * 8:
        nb_all[n * 8 :, :] = jnp.full((nb_all.shape[0] - n * 8, 128), -1.0, F32)
    nb_all[pl.ds(pl.multiple_of(f * 8, 8), 8), :] = nb_send[...]
    og_all[mine, :] = og[...]
    picks[...] = jnp.where(
        lax.broadcasted_iota(jnp.int32, (targets, halo), 0) == srows[...], 1.0, 0.0
    ).astype(BF16)
    names = live(nb1_t[...], count1[...])
    for at in range(0, targets, 128):
        tile = jnp.concatenate([names[:, at : at + 128], jnp.zeros((120, 128), F32)], axis=0)
        nb1[at : at + 128, :] = jnp.transpose(tile)

    pl.semaphore_wait(barrier, n - 1 + parts - 1)

    pair = f + 1 - 2 * lax.rem(f, 2)
    outer = n // 2

    def held(buffer, owner):
        return buffer.at[pl.ds(pl.multiple_of(owner * own, own), own)]

    def gather(source, buffer, sends, recvs):
        first_hop = [
            pltpu.make_async_remote_copy(
                source, held(buffer, f), sends.at[0, i], recvs.at[0, i],
                device_id={"feat": lax.rem(f + 2 * i, n)}, device_id_type=MESH,
            )
            for i in range(1, outer)
        ]
        to_mate = [
            pltpu.make_async_remote_copy(
                source, held(buffer, f), sends.at[1, 0], recvs.at[1, 0],
                device_id={"feat": pair}, device_id_type=MESH,
            )
        ]
        for copy in first_hop + to_mate:
            copy.start()

        def onward():
            for i in range(1, outer):
                first_hop[i - 1].wait_recv()
                owner = held(buffer, lax.rem(f + n - 2 * i, n))
                copy = pltpu.make_async_remote_copy(
                    owner, owner, sends.at[1, i], recvs.at[1, i],
                    device_id={"feat": pair}, device_id_type=MESH,
                )
                copy.start()
                to_mate.append(copy)

        def finish():
            for copy in first_hop:
                copy.wait_send()
            for copy in to_mate:
                copy.wait()

        return onward, finish

    nb_copies = []
    for i in range(1, n):
        copy = pltpu.make_async_remote_copy(
            nb_send, nb_all.at[pl.ds(pl.multiple_of(f * 8, 8), 8)], nb_s.at[i], nb_r.at[i],
            device_id={"feat": lax.rem(f + i, n)}, device_id_type=MESH,
        )
        copy.start()
        nb_copies.append(copy)
    og_onward, og_finish = gather(og, og_all, og_s, og_r)

    blocks = targets // block
    per = block // own
    first = lax.rem(f // per + 1, blocks)

    def send_to(dest):
        return pltpu.make_async_remote_copy(
            part16.at[pl.ds(pl.multiple_of(dest * own, own), own)], rs_buf.at[f],
            rs_s.at[dest], rs_r.at[f], device_id={"feat": dest}, device_id_type=MESH,
        )

    if blocks > 2:
        for copy in loads:
            copy.wait()

    def first_layer(i):
        at = pl.multiple_of(lax.rem(first + i, blocks) * block, block)
        rows = pl.ds(at, block)
        counts_matrix(nb1, at, adj, 0, block, src)
        inv = inverse(nb1[rows, :8])
        total = jnp.zeros((block, hid), F32)
        for j, (lane, size) in enumerate(cols):
            if blocks <= 2 and i == 0:
                loads[j].wait()
                if j == 0:
                    loads[-1].wait()
            chunk = slice(lane, lane + size)
            value = dot(adj[...], face[:, chunk]) * inv + face[rows, chunk].astype(F32)
            value = value.astype(BF16)
            agg[rows, chunk] = value
            total = total + dot(value, w1[chunk, :])
        part32[rows, :] = total
        part16[rows, :] = total.astype(BF16)
        for j in range(per):
            dest = lax.rem(first + i, blocks) * per + j
            pl.when(dest != f)(lambda dest=dest: send_to(dest).start())

    if blocks <= 2:
        first_layer(0)
        og_onward()
        for i in range(1, blocks):
            first_layer(i)
    else:
        pl.loop(0, blocks)(first_layer)
        og_onward()

    for copy in nb_copies:
        copy.wait()
    for at in range(0, nb_all.shape[0], 128):
        turned = jnp.transpose(nb_all[at : at + 128, :])
        for j in range(min(16, n - at // 8)):
            t = at // 8 + j
            nb_nat[t * own : (t + 1) * own, :8] = turned[:own, j * 8 : j * 8 + 8]
    counts_matrix(nb_nat, 0, smat, 0, targets, full)
    picks_t[...] = jnp.transpose(picks[...])

    value = part32[mine, :] + b1[...]
    for i in range(1, n):
        source = lax.rem(f + i, n)
        pltpu.make_async_remote_copy(
            part16.at[pl.ds(0, own)], rs_buf.at[source], rs_s.at[source], rs_r.at[source],
            device_id={"feat": source}, device_id_type=MESH,
        ).wait_recv()
        value = value + rs_buf[source].astype(F32)
    pre_own[...] = value.astype(BF16)
    pre_all[mine, :] = value.astype(BF16)
    onward, finish = gather(pre_own, pre_all, ag_s, ag_r)

    for copy in late:
        copy.wait()
    og_finish()

    def out_part(i):
        rows = pl.ds(pl.multiple_of(i * block, block), block)
        grad_act[rows if blocks <= 2 else slice(None), :] = dot_last(og_all[rows, :], wout[...])

    if blocks <= 2:
        steps(blocks, out_part)
    for lane, size in split(full, 128):
        smat_t[lane : lane + size, :] = jnp.transpose(smat[:, lane : lane + size])
    onward()
    for lane, size in cols:
        agg_t[lane : lane + size, :] = jnp.transpose(agg[:, lane : lane + size])
    finish()

    def hidden_part(i):
        rows = pl.ds(pl.multiple_of(i * block, block), block)
        value = pre_all[rows, :].astype(F32)
        ext[rows, :] = (value * sigmoid(value)).astype(BF16)

    steps(blocks, hidden_part)
    halo_out[...] = dot(picks_t[...], ext[:targets, :]).astype(BF16)
    halo_copy = pltpu.make_async_remote_copy(
        halo_out, ext.at[pl.ds(targets, halo)], halo_sem.at[0], halo_sem.at[1],
        device_id={"dp": lax.rem(d + 1, parts)}, device_id_type=MESH,
    )
    halo_copy.start()

    def neighbour_part(i):
        rows = pl.ds(pl.multiple_of(i * block, block), block)
        gagg[rows, :] = dot(smat[rows, :targets], ext[:targets, :])

    steps(blocks, neighbour_part)
    halo_copy.wait()

    def second_layer(i):
        rows = pl.ds(pl.multiple_of(i * block, block), block)
        inv = inverse(nb_nat[rows, :8])
        if blocks > 2:
            out_part(i)
        total = gagg[rows, :] + dot(smat[rows, targets:], ext[targets:, :])
        value = (ext[rows, :].astype(F32) + total * inv).astype(BF16)
        agg2[rows, :] = value
        step = (grad_act[rows if blocks <= 2 else slice(None), :] * slope(dot(value, win[...]))).astype(BF16)
        back = dot_last(step, win[...])
        gagg[rows, :] = back
        gscaled[rows, :] = (back * inv).astype(BF16)

    steps(blocks, second_layer)

    back_out[...] = dot(smat_t[targets:, :], gscaled[...]).astype(BF16)
    back_copy = pltpu.make_async_remote_copy(
        back_out, back_in, back_sem.at[0], back_sem.at[1],
        device_id={"dp": lax.rem(d + parts - 1, parts)}, device_id_type=MESH,
    )
    back_copy.start()

    for at, size in split(targets, 512):
        rows = slice(at, at + size)
        gtotal[rows, :] = (
            og_all[rows, :].astype(F32) + gagg[rows, :] + dot(smat_t[rows, :], gscaled[...])
        )
    value = dot(agg2[mine, :], win[...])
    act = (value * sigmoid(value)).astype(BF16)
    embed[...] = (ext[mine, :].astype(F32) + dot(act, wout[...])).astype(BF16)

    back_copy.wait()

    def first_gradient(i):
        rows = pl.ds(pl.multiple_of(i * block, block), block)
        value = gtotal[rows, :] + dot(picks[rows, :], back_in[...])
        gp[rows, :] = (value * slope(pre_all[rows, :].astype(F32))).astype(BF16)

    steps(blocks, first_gradient)

    half = width // 2
    size = half // chunks
    side = lax.rem(d, 2)
    chip = d // 2
    chips = parts // 2
    mate = d + 1 - 2 * side

    def place(which, c):
        return pl.ds(pl.multiple_of(which * half + c * size, 16), size)

    pair_copies, chip_copies, end_copies = [], [], []
    for c in range(chunks):
        span = slice(c * size, (c + 1) * size)
        pair_out[span, :] = dot(agg_t[place(1 - side, c), :], gp[...]).astype(BF16)
        copy = pltpu.make_async_remote_copy(
            pair_out.at[pl.ds(c * size, size)], pair_in.at[pl.ds(c * size, size)], pa_s.at[c], pa_r.at[c],
            device_id={"dp": mate}, device_id_type=MESH,
        )
        copy.start()
        pair_copies.append(copy)
    for c in range(chunks):
        span = slice(c * size, (c + 1) * size)
        value = dot(agg_t[place(side, c), :], gp[...])
        pair_copies[c].wait()
        chip_buf[chip, span, :] = (value + pair_in[span, :].astype(F32)).astype(BF16)
        for i in range(1, chips):
            here = chip_buf.at[chip, pl.ds(c * size, size)]
            copy = pltpu.make_async_remote_copy(
                here, here, x_s.at[i, c], x_r.at[i, c],
                device_id={"dp": lax.rem(d + 2 * i, parts)}, device_id_type=MESH,
            )
            copy.start()
            chip_copies.append(copy)
    for c in range(chunks):
        span = slice(c * size, (c + 1) * size)
        for copy in chip_copies[c * (chips - 1) : (c + 1) * (chips - 1)]:
            copy.wait()
        total = chip_buf[0, span, :].astype(F32)
        for i in range(1, chips):
            total = total + chip_buf[i, span, :].astype(F32)
        grad[place(side, c), :] = total.astype(BF16)
        there = grad.at[place(side, c)]
        copy = pltpu.make_async_remote_copy(
            there, there, pb_s.at[c], pb_r.at[c], device_id={"dp": mate}, device_id_type=MESH,
        )
        copy.start()
        end_copies.append(copy)
    for copy in end_copies:
        copy.wait()
    for i in range(1, n):
        send_to(lax.rem(f + i, n)).wait_send()


def finish_kernel(embed_in, grad_in, embed, grad, narrow, wide, in_sem, out_sem):
    rows, pieces = grad_in.shape[0], in_sem.shape[0] - 1
    size = rows // pieces
    small = pltpu.make_async_copy(embed_in, embed, in_sem.at[pieces])
    small.start()

    def part(ref, i):
        return ref.at[pl.ds(i * size, size)]

    arrive = [
        pltpu.make_async_copy(part(grad_in, i), part(narrow, i), in_sem.at[i]) for i in range(pieces)
    ]
    leave = [pltpu.make_async_copy(part(wide, i), part(grad, i), out_sem.at[i]) for i in range(pieces)]
    for copy in arrive:
        copy.start()
    for i in range(pieces):
        arrive[i].wait()
        span = slice(i * size, (i + 1) * size)
        wide[span, :] = narrow[span, :].astype(F32)
        leave[i].start()
    small.wait()
    for copy in leave:
        copy.wait()


def finished(embed, grad):
    pieces = next(c for c in (4, 2, 1) if (grad.shape[0] // c) % 16 == 0)
    any_space = pl.BlockSpec(memory_space=pl.ANY)
    return pl.pallas_call(
        finish_kernel,
        out_shape=(
            jax.ShapeDtypeStruct(embed.shape, BF16),
            jax.ShapeDtypeStruct(grad.shape, F32),
        ),
        in_specs=[any_space, any_space],
        out_specs=(any_space, any_space),
        scratch_shapes=[
            pltpu.VMEM(grad.shape, BF16),
            pltpu.VMEM(grad.shape, F32),
            pltpu.SemaphoreType.DMA((pieces + 1,)),
            pltpu.SemaphoreType.DMA((pieces,)),
        ],
        compiler_params=pltpu.CompilerParams(vmem_limit_bytes=56 * 1024 * 1024),
        name="finish",
    )(embed, grad)


def fused(
    n, parts, face_grid, nb1, count1, w_first, b_first, send_rows, nb2, count2, w_in, w_out, out_grad
):
    src, width = face_grid.shape
    targets, hid = nb1.shape[1], w_first.shape[1]
    inner = w_in.shape[1]
    own, halo = nb2.shape[1], send_rows.shape[1]
    full = targets + halo
    block = min(targets, 256)
    half = width // 2
    chunks = next(c for c in (4, 2, 1) if (half // c) % 16 == 0)
    chips = parts // 2
    tiles = -(-n * 8 // 128) * 128
    any_space = pl.BlockSpec(memory_space=pl.ANY)
    vmem = pl.BlockSpec(memory_space=pltpu.VMEM)
    dma = pltpu.SemaphoreType.DMA
    return pl.pallas_call(
        functools.partial(kernel, n, parts, block, chunks),
        out_shape=(
            jax.ShapeDtypeStruct((own, hid), BF16),
            jax.ShapeDtypeStruct((width, hid), BF16),
        ),
        in_specs=[
            any_space, vmem, vmem, any_space, vmem, vmem, vmem, vmem, any_space, any_space, vmem,
        ],
        out_specs=(vmem, vmem),
        scratch_shapes=[
            pltpu.VMEM((src, width), BF16),
            pltpu.VMEM((width, hid), BF16),
            pltpu.VMEM((hid, inner), BF16),
            pltpu.VMEM((inner, hid), BF16),
            pltpu.VMEM((block, src), BF16),
            pltpu.VMEM((targets, width), BF16),
            pltpu.VMEM((width, targets), BF16),
            pltpu.VMEM((targets, hid), F32),
            pltpu.VMEM((targets, hid), BF16),
            pltpu.VMEM((n, own, hid), BF16),
            pltpu.VMEM((own, hid), BF16),
            pltpu.VMEM((targets, hid), BF16),
            pltpu.VMEM((full, hid), BF16),
            pltpu.VMEM((targets, halo), BF16),
            pltpu.VMEM((halo, targets), BF16),
            pltpu.VMEM((targets, hid), BF16),
            pltpu.VMEM((targets, 128), F32),
            pltpu.VMEM((8, 128), F32),
            pltpu.VMEM((tiles, 128), F32),
            pltpu.VMEM((targets, 128), F32),
            pltpu.VMEM((targets, full), BF16),
            pltpu.VMEM((full, targets), BF16),
            pltpu.VMEM((targets if targets // block <= 2 else block, inner), F32),
            pltpu.VMEM((targets, hid), BF16),
            pltpu.VMEM((targets, hid), BF16),
            pltpu.VMEM((targets, hid), F32),
            pltpu.VMEM((halo, hid), BF16),
            pltpu.VMEM((halo, hid), BF16),
            pltpu.VMEM((halo, hid), BF16),
            pltpu.VMEM((targets, hid), F32),
            pltpu.VMEM((targets, hid), BF16),
            pltpu.VMEM((half, hid), BF16),
            pltpu.VMEM((half, hid), BF16),
            pltpu.VMEM((chips, half, hid), BF16),
            dma((len(split(width, 256)) + 3,)),
            dma((n,)), dma((n,)),
            dma((2, n // 2)), dma((2, n // 2)), dma((2, n // 2)), dma((2, n // 2)),
            dma((n,)), dma((n,)),
            dma((2,)), dma((2,)),
            dma((chunks,)), dma((chunks,)),
            dma((chips, chunks)), dma((chips, chunks)),
            dma((chunks,)), dma((chunks,)),
        ],
        compiler_params=pltpu.CompilerParams(
            collective_id=0, has_side_effects=True, vmem_limit_bytes=60 * 1024 * 1024
        ),
        cost_estimate=pl.CostEstimate(
            flops=2 * targets * src * width, bytes_accessed=2 * src * width, transcendentals=0
        ),
        name="fused_step",
    )(
        face_grid, nb1, count1, w_first, b_first, send_rows, nb2, count2, w_in, w_out, out_grad
    )


def solution(mesh):
    n, parts = mesh.shape["feat"], mesh.shape["dp"]

    def body(
        face_grid, first_nbrs, first_count, w_first, b_first, send_rows,
        second_nbrs, second_count, w_in, w_out, out_grad,
    ):
        embed, grad = fused(
            n, parts, face_grid, first_nbrs.T, first_count.reshape(1, -1), w_first,
            b_first.reshape(1, -1), send_rows.reshape(1, -1), second_nbrs.T,
            second_count.reshape(1, -1), w_in, w_out, out_grad,
        )
        return finished(embed, grad)

    return jax.shard_map(
        body,
        mesh=mesh,
        in_specs=(
            P("dp", "feat"), P("dp", None), P("dp"), P("feat", None), P(), P("dp"),
            P(("dp", "feat"), None), P(("dp", "feat")), P(), P(), P(("dp", "feat"), None),
        ),
        out_specs=(P(("dp", "feat"), None), P("feat", None)),
        check_vma=False,
    )
```

```python
import functools

import jax
import jax.numpy as jnp
from jax import lax
from jax.experimental import pallas as pl
from jax.experimental.pallas import tpu as pltpu
from jax.sharding import PartitionSpec as P

MESH = pl.DeviceIdType.MESH
F32, BF16 = jnp.float32, jnp.bfloat16


def dot(a, b):
    return jnp.dot(a, b, preferred_element_type=F32)


def dot_last(a, b):
    return lax.dot_general(a, b, (((1,), (1,)), ((), ())), preferred_element_type=F32)


def sigmoid(value):
    return 0.5 * jnp.tanh(0.5 * value) + 0.5


def slope(value):
    sig = sigmoid(value)
    return sig * (1.0 + value * (1.0 - sig))


def steps(count, fn):
    if count <= 2:
        for i in range(count):
            fn(i)
    else:
        pl.loop(0, count)(fn)


def split(size, width):
    return [(at, min(width, size - at)) for at in range(0, size, width)]


def counts_matrix(nbrs, source, out, at, rows, width):
    spots = [
        (lane, size, (lax.broadcasted_iota(jnp.int32, (8, size), 1) + lane).astype(F32))
        for lane, size in split(width, 1024)
    ]

    def group(g):
        for lane, size, spot in spots:
            pieces = []
            for piece in range(2):
                names = nbrs[pl.ds(pl.multiple_of(source + g * 16 + piece * 8, 8), 8), :8]
                total = jnp.zeros((8, size), F32)
                for slot in range(8):
                    total = total + jnp.where(names[:, slot : slot + 1] == spot, 1.0, 0.0)
                pieces.append(total)
            here = pl.ds(pl.multiple_of(at + g * 16, 16), 16)
            out[here, lane : lane + size] = jnp.concatenate(pieces, axis=0).astype(BF16)

    several = 4 if width <= 1024 and rows % 64 == 0 else 1

    def groups(i):
        for j in range(several):
            group(i * several + j)

    pl.loop(0, rows // 16 // several)(groups)


def live(nbrs, count):
    slots = lax.broadcasted_iota(jnp.int32, nbrs.shape, 0)
    return jnp.where(slots < count, nbrs, -1).astype(F32)


def inverse(names):
    live = jnp.where(names >= 0, 1.0, 0.0)
    return 1.0 / jnp.sum(live, axis=1, keepdims=True)


def kernel(
    n, parts, block, chunks,
    face_hbm, nb1_t, count1, w1_hbm, b1, srows, nb2_t, count2, win_hbm, wout_hbm, og,
    embed, grad,
    face, w1, win, wout, adj, agg, agg_t, part32, part16, rs_buf, pre_own, pre_all,
    ext, picks, picks_t, og_all, nb1, nb_send, nb_all, nb_nat, smat, smat_t, grad_act, agg2, gscaled, gagg,
    halo_out, back_out, back_in, gtotal, gp, pair_out, pair_in, chip_buf,
    load_sem, rs_s, rs_r, ag_s, ag_r, og_s, og_r, nb_s, nb_r, halo_sem, back_sem,
    pa_s, pa_r, x_s, x_r, pb_s, pb_r,
):
    f, d = lax.axis_index("feat"), lax.axis_index("dp")
    src, width = face.shape
    targets, hid = nb1.shape[0], w1.shape[1]
    own = og.shape[0]
    halo = srows.shape[1]
    full = targets + halo
    mine = pl.ds(pl.multiple_of(f * own, own), own)
    cols = split(width, 256)

    loads = [
        pltpu.make_async_copy(face_hbm.at[:, pl.ds(at, size)], face.at[:, pl.ds(at, size)], load_sem.at[i])
        for i, (at, size) in enumerate(cols)
    ]
    loads.append(pltpu.make_async_copy(w1_hbm, w1, load_sem.at[len(cols)]))
    late = [
        pltpu.make_async_copy(wout_hbm, wout, load_sem.at[len(cols) + 1]),
        pltpu.make_async_copy(win_hbm, win, load_sem.at[len(cols) + 2]),
    ]
    for copy in loads + late:
        copy.start()

    barrier = pltpu.get_barrier_semaphore()
    for i in range(1, n):
        pl.semaphore_signal(barrier, inc=1, device_id={"feat": lax.rem(f + i, n)}, device_id_type=MESH)
    for i in range(1, parts):
        pl.semaphore_signal(barrier, inc=1, device_id={"dp": lax.rem(d + i, parts)}, device_id_type=MESH)

    nb_send[...] = jnp.full(nb_send.shape, -1.0, F32)
    nb_send[:, :own] = live(nb2_t[...], count2[...])
    if nb_all.shape[0] > n * 8:
        nb_all[n * 8 :, :] = jnp.full((nb_all.shape[0] - n * 8, 128), -1.0, F32)
    nb_all[pl.ds(pl.multiple_of(f * 8, 8), 8), :] = nb_send[...]
    og_all[mine, :] = og[...]
    picks[...] = jnp.where(
        lax.broadcasted_iota(jnp.int32, (targets, halo), 0) == srows[...], 1.0, 0.0
    ).astype(BF16)
    names = live(nb1_t[...], count1[...])
    for at in range(0, targets, 128):
        tile = jnp.concatenate([names[:, at : at + 128], jnp.zeros((120, 128), F32)], axis=0)
        nb1[at : at + 128, :] = jnp.transpose(tile)

    blocks = targets // block
    per = block // own
    first = lax.rem(f // per + 1, blocks)
    counts_matrix(nb1, pl.multiple_of(first * block, block), adj, 0, block, src)

    pl.semaphore_wait(barrier, n - 1 + parts - 1)

    pair = f + 1 - 2 * lax.rem(f, 2)
    outer = n // 2

    def held(buffer, owner):
        return buffer.at[pl.ds(pl.multiple_of(owner * own, own), own)]

    def gather(source, buffer, sends, recvs):
        first_hop = [
            pltpu.make_async_remote_copy(
                source, held(buffer, f), sends.at[0, i], recvs.at[0, i],
                device_id={"feat": lax.rem(f + 2 * i, n)}, device_id_type=MESH,
            )
            for i in range(1, outer)
        ]
        to_mate = [
            pltpu.make_async_remote_copy(
                source, held(buffer, f), sends.at[1, 0], recvs.at[1, 0],
                device_id={"feat": pair}, device_id_type=MESH,
            )
        ]
        for copy in first_hop + to_mate:
            copy.start()

        def onward():
            for i in range(1, outer):
                first_hop[i - 1].wait_recv()
                owner = held(buffer, lax.rem(f + n - 2 * i, n))
                copy = pltpu.make_async_remote_copy(
                    owner, owner, sends.at[1, i], recvs.at[1, i],
                    device_id={"feat": pair}, device_id_type=MESH,
                )
                copy.start()
                to_mate.append(copy)

        def finish():
            for copy in first_hop:
                copy.wait_send()
            for copy in to_mate:
                copy.wait()

        return onward, finish

    nb_copies = []
    for i in range(1, n):
        copy = pltpu.make_async_remote_copy(
            nb_send, nb_all.at[pl.ds(pl.multiple_of(f * 8, 8), 8)], nb_s.at[i], nb_r.at[i],
            device_id={"feat": lax.rem(f + i, n)}, device_id_type=MESH,
        )
        copy.start()
        nb_copies.append(copy)
    og_onward, og_finish = gather(og, og_all, og_s, og_r)

    def send_to(dest):
        return pltpu.make_async_remote_copy(
            part16.at[pl.ds(pl.multiple_of(dest * own, own), own)], rs_buf.at[f],
            rs_s.at[dest], rs_r.at[f], device_id={"feat": dest}, device_id_type=MESH,
        )

    if blocks > 2:
        for copy in loads:
            copy.wait()

    def first_layer(i):
        at = pl.multiple_of(lax.rem(first + i, blocks) * block, block)
        rows = pl.ds(at, block)
        if not isinstance(i, int):
            pl.when(i > 0)(lambda: counts_matrix(nb1, at, adj, 0, block, src))
        elif i > 0:
            counts_matrix(nb1, at, adj, 0, block, src)
        inv = inverse(nb1[rows, :8])
        total = jnp.zeros((block, hid), F32)
        for j, (lane, size) in enumerate(cols):
            if blocks <= 2 and i == 0:
                loads[j].wait()
                if j == 0:
                    loads[-1].wait()
            chunk = slice(lane, lane + size)
            value = dot(adj[...], face[:, chunk]) * inv + face[rows, chunk].astype(F32)
            value = value.astype(BF16)
            agg[rows, chunk] = value
            total = total + dot(value, w1[chunk, :])
        part32[rows, :] = total
        part16[rows, :] = total.astype(BF16)
        for j in range(per):
            dest = lax.rem(first + i, blocks) * per + j
            pl.when(dest != f)(lambda dest=dest: send_to(dest).start())

    if blocks <= 2:
        first_layer(0)
        og_onward()
        for i in range(1, blocks):
            first_layer(i)
    else:
        pl.loop(0, blocks)(first_layer)
        og_onward()

    for copy in nb_copies:
        copy.wait()
    for at in range(0, nb_all.shape[0], 128):
        turned = jnp.transpose(nb_all[at : at + 128, :])
        for j in range(min(16, n - at // 8)):
            t = at // 8 + j
            nb_nat[t * own : (t + 1) * own, :8] = turned[:own, j * 8 : j * 8 + 8]
    counts_matrix(nb_nat, 0, smat, 0, targets, full)
    picks_t[...] = jnp.transpose(picks[...])
    for copy in late:
        copy.wait()
    og_finish()

    def out_part(i):
        rows = pl.ds(pl.multiple_of(i * block, block), block)
        grad_act[rows if blocks <= 2 else slice(None), :] = dot_last(og_all[rows, :], wout[...])

    if blocks <= 2:
        steps(blocks, out_part)
    for lane, size in split(full, 128):
        smat_t[lane : lane + size, :] = jnp.transpose(smat[:, lane : lane + size])

    value = part32[mine, :] + b1[...]
    for i in range(1, n):
        source = lax.rem(f + i, n)
        pltpu.make_async_remote_copy(
            part16.at[pl.ds(0, own)], rs_buf.at[source], rs_s.at[source], rs_r.at[source],
            device_id={"feat": source}, device_id_type=MESH,
        ).wait_recv()
        value = value + rs_buf[source].astype(F32)
    pre_own[...] = value.astype(BF16)
    pre_all[mine, :] = value.astype(BF16)
    onward, finish = gather(pre_own, pre_all, ag_s, ag_r)

    onward()
    early = (len(cols) + 1) // 2
    for lane, size in cols[:early]:
        agg_t[lane : lane + size, :] = jnp.transpose(agg[:, lane : lane + size])
    finish()

    def hidden_part(i):
        rows = pl.ds(pl.multiple_of(i * block, block), block)
        value = pre_all[rows, :].astype(F32)
        ext[rows, :] = (value * sigmoid(value)).astype(BF16)

    steps(blocks, hidden_part)
    halo_out[...] = dot(picks_t[...], ext[:targets, :]).astype(BF16)
    halo_copy = pltpu.make_async_remote_copy(
        halo_out, ext.at[pl.ds(targets, halo)], halo_sem.at[0], halo_sem.at[1],
        device_id={"dp": lax.rem(d + 1, parts)}, device_id_type=MESH,
    )
    halo_copy.start()

    def neighbour_part(i):
        rows = pl.ds(pl.multiple_of(i * block, block), block)
        gagg[rows, :] = dot(smat[rows, :targets], ext[:targets, :])

    steps(blocks, neighbour_part)
    for lane, size in cols[early:]:
        agg_t[lane : lane + size, :] = jnp.transpose(agg[:, lane : lane + size])
    halo_copy.wait()

    def second_layer(i):
        rows = pl.ds(pl.multiple_of(i * block, block), block)
        inv = inverse(nb_nat[rows, :8])
        if blocks > 2:
            out_part(i)
        total = gagg[rows, :] + dot(smat[rows, targets:], ext[targets:, :])
        value = (ext[rows, :].astype(F32) + total * inv).astype(BF16)
        agg2[rows, :] = value
        step = (grad_act[rows if blocks <= 2 else slice(None), :] * slope(dot(value, win[...]))).astype(BF16)
        back = dot_last(step, win[...])
        gagg[rows, :] = back
        gscaled[rows, :] = (back * inv).astype(BF16)

    steps(blocks, second_layer)

    back_out[...] = dot(smat_t[targets:, :], gscaled[...]).astype(BF16)
    back_copy = pltpu.make_async_remote_copy(
        back_out, back_in, back_sem.at[0], back_sem.at[1],
        device_id={"dp": lax.rem(d + parts - 1, parts)}, device_id_type=MESH,
    )
    back_copy.start()

    for at, size in split(targets, 512):
        rows = slice(at, at + size)
        gtotal[rows, :] = (
            og_all[rows, :].astype(F32) + gagg[rows, :] + dot(smat_t[rows, :], gscaled[...])
        )
    value = dot(agg2[mine, :], win[...])
    act = (value * sigmoid(value)).astype(BF16)
    embed[...] = (ext[mine, :].astype(F32) + dot(act, wout[...])).astype(BF16)

    back_copy.wait()

    def first_gradient(i):
        rows = pl.ds(pl.multiple_of(i * block, block), block)
        value = gtotal[rows, :] + dot(picks[rows, :], back_in[...])
        gp[rows, :] = (value * slope(pre_all[rows, :].astype(F32))).astype(BF16)

    steps(blocks, first_gradient)

    half = width // 2
    size = half // chunks
    side = lax.rem(d, 2)
    chip = d // 2
    chips = parts // 2
    mate = d + 1 - 2 * side

    def place(which, c):
        return pl.ds(pl.multiple_of(which * half + c * size, 16), size)

    pair_copies, chip_copies, end_copies = [], [], []
    for c in range(chunks):
        span = slice(c * size, (c + 1) * size)
        pair_out[span, :] = dot(agg_t[place(1 - side, c), :], gp[...]).astype(BF16)
        copy = pltpu.make_async_remote_copy(
            pair_out.at[pl.ds(c * size, size)], pair_in.at[pl.ds(c * size, size)], pa_s.at[c], pa_r.at[c],
            device_id={"dp": mate}, device_id_type=MESH,
        )
        copy.start()
        pair_copies.append(copy)
    for c in range(chunks):
        span = slice(c * size, (c + 1) * size)
        value = dot(agg_t[place(side, c), :], gp[...])
        pair_copies[c].wait()
        chip_buf[chip, span, :] = (value + pair_in[span, :].astype(F32)).astype(BF16)
        for i in range(1, chips):
            here = chip_buf.at[chip, pl.ds(c * size, size)]
            copy = pltpu.make_async_remote_copy(
                here, here, x_s.at[i, c], x_r.at[i, c],
                device_id={"dp": lax.rem(d + 2 * i, parts)}, device_id_type=MESH,
            )
            copy.start()
            chip_copies.append(copy)
    for c in range(chunks):
        span = slice(c * size, (c + 1) * size)
        for copy in chip_copies[c * (chips - 1) : (c + 1) * (chips - 1)]:
            copy.wait()
        total = chip_buf[0, span, :].astype(F32)
        for i in range(1, chips):
            total = total + chip_buf[i, span, :].astype(F32)
        grad[place(side, c), :] = total.astype(BF16)
        there = grad.at[place(side, c)]
        copy = pltpu.make_async_remote_copy(
            there, there, pb_s.at[c], pb_r.at[c], device_id={"dp": mate}, device_id_type=MESH,
        )
        copy.start()
        end_copies.append(copy)
    for copy in end_copies:
        copy.wait()
    for i in range(1, n):
        send_to(lax.rem(f + i, n)).wait_send()


def finish_kernel(embed_in, grad_in, embed, grad, narrow, wide, in_sem, out_sem):
    rows, pieces = grad_in.shape[0], in_sem.shape[0] - 1
    size = rows // pieces
    small = pltpu.make_async_copy(embed_in, embed, in_sem.at[pieces])
    small.start()

    def part(ref, i):
        return ref.at[pl.ds(i * size, size)]

    arrive = [
        pltpu.make_async_copy(part(grad_in, i), part(narrow, i), in_sem.at[i]) for i in range(pieces)
    ]
    leave = [pltpu.make_async_copy(part(wide, i), part(grad, i), out_sem.at[i]) for i in range(pieces)]
    for copy in arrive:
        copy.start()
    for i in range(pieces):
        arrive[i].wait()
        span = slice(i * size, (i + 1) * size)
        wide[span, :] = narrow[span, :].astype(F32)
        leave[i].start()
    small.wait()
    for copy in leave:
        copy.wait()


def finished(embed, grad):
    pieces = next(c for c in (4, 2, 1) if (grad.shape[0] // c) % 16 == 0)
    any_space = pl.BlockSpec(memory_space=pl.ANY)
    return pl.pallas_call(
        finish_kernel,
        out_shape=(
            jax.ShapeDtypeStruct(embed.shape, BF16),
            jax.ShapeDtypeStruct(grad.shape, F32),
        ),
        in_specs=[any_space, any_space],
        out_specs=(any_space, any_space),
        scratch_shapes=[
            pltpu.VMEM(grad.shape, BF16),
            pltpu.VMEM(grad.shape, F32),
            pltpu.SemaphoreType.DMA((pieces + 1,)),
            pltpu.SemaphoreType.DMA((pieces,)),
        ],
        compiler_params=pltpu.CompilerParams(vmem_limit_bytes=56 * 1024 * 1024),
        name="finish",
    )(embed, grad)


def fused(
    n, parts, face_grid, nb1, count1, w_first, b_first, send_rows, nb2, count2, w_in, w_out, out_grad
):
    src, width = face_grid.shape
    targets, hid = nb1.shape[1], w_first.shape[1]
    inner = w_in.shape[1]
    own, halo = nb2.shape[1], send_rows.shape[1]
    full = targets + halo
    block = min(targets, 256)
    half = width // 2
    chunks = next(c for c in (4, 2, 1) if (half // c) % 16 == 0)
    chips = parts // 2
    tiles = -(-n * 8 // 128) * 128
    any_space = pl.BlockSpec(memory_space=pl.ANY)
    vmem = pl.BlockSpec(memory_space=pltpu.VMEM)
    dma = pltpu.SemaphoreType.DMA
    return pl.pallas_call(
        functools.partial(kernel, n, parts, block, chunks),
        out_shape=(
            jax.ShapeDtypeStruct((own, hid), BF16),
            jax.ShapeDtypeStruct((width, hid), BF16),
        ),
        in_specs=[
            any_space, vmem, vmem, any_space, vmem, vmem, vmem, vmem, any_space, any_space, vmem,
        ],
        out_specs=(vmem, vmem),
        scratch_shapes=[
            pltpu.VMEM((src, width), BF16),
            pltpu.VMEM((width, hid), BF16),
            pltpu.VMEM((hid, inner), BF16),
            pltpu.VMEM((inner, hid), BF16),
            pltpu.VMEM((block, src), BF16),
            pltpu.VMEM((targets, width), BF16),
            pltpu.VMEM((width, targets), BF16),
            pltpu.VMEM((targets, hid), F32),
            pltpu.VMEM((targets, hid), BF16),
            pltpu.VMEM((n, own, hid), BF16),
            pltpu.VMEM((own, hid), BF16),
            pltpu.VMEM((targets, hid), BF16),
            pltpu.VMEM((full, hid), BF16),
            pltpu.VMEM((targets, halo), BF16),
            pltpu.VMEM((halo, targets), BF16),
            pltpu.VMEM((targets, hid), BF16),
            pltpu.VMEM((targets, 128), F32),
            pltpu.VMEM((8, 128), F32),
            pltpu.VMEM((tiles, 128), F32),
            pltpu.VMEM((targets, 128), F32),
            pltpu.VMEM((targets, full), BF16),
            pltpu.VMEM((full, targets), BF16),
            pltpu.VMEM((targets if targets // block <= 2 else block, inner), F32),
            pltpu.VMEM((targets, hid), BF16),
            pltpu.VMEM((targets, hid), BF16),
            pltpu.VMEM((targets, hid), F32),
            pltpu.VMEM((halo, hid), BF16),
            pltpu.VMEM((halo, hid), BF16),
            pltpu.VMEM((halo, hid), BF16),
            pltpu.VMEM((targets, hid), F32),
            pltpu.VMEM((targets, hid), BF16),
            pltpu.VMEM((half, hid), BF16),
            pltpu.VMEM((half, hid), BF16),
            pltpu.VMEM((chips, half, hid), BF16),
            dma((len(split(width, 256)) + 3,)),
            dma((n,)), dma((n,)),
            dma((2, n // 2)), dma((2, n // 2)), dma((2, n // 2)), dma((2, n // 2)),
            dma((n,)), dma((n,)),
            dma((2,)), dma((2,)),
            dma((chunks,)), dma((chunks,)),
            dma((chips, chunks)), dma((chips, chunks)),
            dma((chunks,)), dma((chunks,)),
        ],
        compiler_params=pltpu.CompilerParams(
            collective_id=0, has_side_effects=True, vmem_limit_bytes=60 * 1024 * 1024
        ),
        cost_estimate=pl.CostEstimate(
            flops=2 * targets * src * width, bytes_accessed=2 * src * width, transcendentals=0
        ),
        name="fused_step",
    )(
        face_grid, nb1, count1, w_first, b_first, send_rows, nb2, count2, w_in, w_out, out_grad
    )


def solution(mesh):
    n, parts = mesh.shape["feat"], mesh.shape["dp"]

    def body(
        face_grid, first_nbrs, first_count, w_first, b_first, send_rows,
        second_nbrs, second_count, w_in, w_out, out_grad,
    ):
        embed, grad = fused(
            n, parts, face_grid, first_nbrs.T, first_count.reshape(1, -1), w_first,
            b_first.reshape(1, -1), send_rows.reshape(1, -1), second_nbrs.T,
            second_count.reshape(1, -1), w_in, w_out, out_grad,
        )
        return finished(embed, grad)

    return jax.shard_map(
        body,
        mesh=mesh,
        in_specs=(
            P("dp", "feat"), P("dp", None), P("dp"), P("feat", None), P(), P("dp"),
            P(("dp", "feat"), None), P(("dp", "feat")), P(), P(), P(("dp", "feat"), None),
        ),
        out_specs=(P(("dp", "feat"), None), P("feat", None)),
        check_vma=False,
    )
```

```python
import functools

import jax
import jax.numpy as jnp
from jax import lax
from jax.experimental import pallas as pl
from jax.experimental.pallas import tpu as pltpu
from jax.sharding import PartitionSpec as P

MESH = pl.DeviceIdType.MESH
F32, BF16 = jnp.float32, jnp.bfloat16


def dot(a, b):
    return jnp.dot(a, b, preferred_element_type=F32)


def dot_last(a, b):
    return lax.dot_general(a, b, (((1,), (1,)), ((), ())), preferred_element_type=F32)


def sigmoid(value):
    return 0.5 * jnp.tanh(0.5 * value) + 0.5


def slope(value):
    sig = sigmoid(value)
    return sig * (1.0 + value * (1.0 - sig))


def steps(count, fn):
    if count <= 2:
        for i in range(count):
            fn(i)
    else:
        pl.loop(0, count)(fn)


def split(size, width):
    return [(at, min(width, size - at)) for at in range(0, size, width)]


def counts_matrix(nbrs, source, out, at, rows, width):
    spots = [
        (lane, size, (lax.broadcasted_iota(jnp.int32, (8, size), 1) + lane).astype(F32))
        for lane, size in split(width, 1024)
    ]

    def group(g):
        for lane, size, spot in spots:
            pieces = []
            for piece in range(2):
                names = nbrs[pl.ds(pl.multiple_of(source + g * 16 + piece * 8, 8), 8), :8]
                total = jnp.zeros((8, size), F32)
                for slot in range(8):
                    total = total + jnp.where(names[:, slot : slot + 1] == spot, 1.0, 0.0)
                pieces.append(total)
            here = pl.ds(pl.multiple_of(at + g * 16, 16), 16)
            out[here, lane : lane + size] = jnp.concatenate(pieces, axis=0).astype(BF16)

    several = 4 if width <= 1024 and rows % 64 == 0 else 1

    def groups(i):
        for j in range(several):
            group(i * several + j)

    pl.loop(0, rows // 16 // several)(groups)


def live(nbrs, count):
    slots = lax.broadcasted_iota(jnp.int32, nbrs.shape, 0)
    return jnp.where(slots < count, nbrs, -1).astype(F32)


def inverse(names):
    live = jnp.where(names >= 0, 1.0, 0.0)
    return 1.0 / jnp.sum(live, axis=1, keepdims=True)


def kernel(
    n, parts, block, chunks,
    face_hbm, nb1_t, count1, w1_hbm, b1, srows, nb2_t, count2, win_hbm, wout_hbm, og,
    embed, grad,
    face, w1, win, wout, adj, agg, agg_t, part32, part16, rs_buf, pre_own, pre_all,
    ext, picks, picks_t, og_all, nb1, nb_send, nb_all, nb_nat, smat, smat_t, grad_act, agg2, gscaled, gagg,
    halo_out, back_out, back_in, gtotal, gp, pair_out, pair_in, chip_buf,
    load_sem, rs_s, rs_r, ag_s, ag_r, og_s, og_r, nb_s, nb_r, halo_sem, back_sem,
    pa_s, pa_r, x_s, x_r, pb_s, pb_r,
):
    f, d = lax.axis_index("feat"), lax.axis_index("dp")
    src, width = face.shape
    targets, hid = nb1.shape[0], w1.shape[1]
    own = og.shape[0]
    halo = srows.shape[1]
    full = targets + halo
    mine = pl.ds(pl.multiple_of(f * own, own), own)
    cols = split(width, 256)

    loads = [
        pltpu.make_async_copy(face_hbm.at[:, pl.ds(at, size)], face.at[:, pl.ds(at, size)], load_sem.at[i])
        for i, (at, size) in enumerate(cols)
    ]
    loads.append(pltpu.make_async_copy(w1_hbm, w1, load_sem.at[len(cols)]))
    late = [
        pltpu.make_async_copy(wout_hbm, wout, load_sem.at[len(cols) + 1]),
        pltpu.make_async_copy(win_hbm, win, load_sem.at[len(cols) + 2]),
    ]
    for copy in loads + late:
        copy.start()

    barrier = pltpu.get_barrier_semaphore()
    for i in range(1, n):
        pl.semaphore_signal(barrier, inc=1, device_id={"feat": lax.rem(f + i, n)}, device_id_type=MESH)
    for i in range(1, parts):
        pl.semaphore_signal(barrier, inc=1, device_id={"dp": lax.rem(d + i, parts)}, device_id_type=MESH)

    nb_send[...] = jnp.full(nb_send.shape, -1.0, F32)
    nb_send[:, :own] = live(nb2_t[...], count2[...])
    if nb_all.shape[0] > n * 8:
        nb_all[n * 8 :, :] = jnp.full((nb_all.shape[0] - n * 8, 128), -1.0, F32)
    nb_all[pl.ds(pl.multiple_of(f * 8, 8), 8), :] = nb_send[...]
    og_all[mine, :] = og[...]
    picks[...] = jnp.where(
        lax.broadcasted_iota(jnp.int32, (targets, halo), 0) == srows[...], 1.0, 0.0
    ).astype(BF16)
    names = live(nb1_t[...], count1[...])
    for at in range(0, targets, 128):
        tile = jnp.concatenate([names[:, at : at + 128], jnp.zeros((120, 128), F32)], axis=0)
        nb1[at : at + 128, :] = jnp.transpose(tile)

    blocks = targets // block
    per = block // own
    first = lax.rem(f // per + 1, blocks)
    counts_matrix(nb1, pl.multiple_of(first * block, block), adj, 0, block, src)

    pl.semaphore_wait(barrier, n - 1 + parts - 1)

    pair = f + 1 - 2 * lax.rem(f, 2)
    outer = n // 2

    def held(buffer, owner):
        return buffer.at[pl.ds(pl.multiple_of(owner * own, own), own)]

    def gather(source, buffer, sends, recvs):
        first_hop = [
            pltpu.make_async_remote_copy(
                source, held(buffer, f), sends.at[0, i], recvs.at[0, i],
                device_id={"feat": lax.rem(f + 2 * i, n)}, device_id_type=MESH,
            )
            for i in range(1, outer)
        ]
        to_mate = [
            pltpu.make_async_remote_copy(
                source, held(buffer, f), sends.at[1, 0], recvs.at[1, 0],
                device_id={"feat": pair}, device_id_type=MESH,
            )
        ]
        for copy in first_hop + to_mate:
            copy.start()

        def onward():
            for i in range(1, outer):
                first_hop[i - 1].wait_recv()
                owner = held(buffer, lax.rem(f + n - 2 * i, n))
                copy = pltpu.make_async_remote_copy(
                    owner, owner, sends.at[1, i], recvs.at[1, i],
                    device_id={"feat": pair}, device_id_type=MESH,
                )
                copy.start()
                to_mate.append(copy)

        def finish():
            for copy in first_hop:
                copy.wait_send()
            for copy in to_mate:
                copy.wait()

        return onward, finish

    nb_copies = []
    for i in range(1, n):
        copy = pltpu.make_async_remote_copy(
            nb_send, nb_all.at[pl.ds(pl.multiple_of(f * 8, 8), 8)], nb_s.at[i], nb_r.at[i],
            device_id={"feat": lax.rem(f + i, n)}, device_id_type=MESH,
        )
        copy.start()
        nb_copies.append(copy)
    og_onward, og_finish = gather(og, og_all, og_s, og_r)

    def send_to(dest):
        return pltpu.make_async_remote_copy(
            part16.at[pl.ds(pl.multiple_of(dest * own, own), own)], rs_buf.at[f],
            rs_s.at[dest], rs_r.at[f], device_id={"feat": dest}, device_id_type=MESH,
        )

    if blocks > 2:
        for copy in loads:
            copy.wait()

    def first_layer(i):
        at = pl.multiple_of(lax.rem(first + i, blocks) * block, block)
        rows = pl.ds(at, block)
        if not isinstance(i, int):
            pl.when(i > 0)(lambda: counts_matrix(nb1, at, adj, 0, block, src))
        elif i > 0:
            counts_matrix(nb1, at, adj, 0, block, src)
        inv = inverse(nb1[rows, :8])
        total = jnp.zeros((block, hid), F32)
        for j, (lane, size) in enumerate(cols):
            if blocks <= 2 and i == 0:
                loads[j].wait()
                if j == 0:
                    loads[-1].wait()
            chunk = slice(lane, lane + size)
            value = dot(adj[...], face[:, chunk]) * inv + face[rows, chunk].astype(F32)
            value = value.astype(BF16)
            agg[rows, chunk] = value
            total = total + dot(value, w1[chunk, :])
        part32[rows, :] = total
        part16[rows, :] = total.astype(BF16)
        for j in range(per):
            dest = lax.rem(first + i, blocks) * per + j
            pl.when(dest != f)(lambda dest=dest: send_to(dest).start())

    if blocks <= 2:
        for i in range(blocks):
            first_layer(i)
    else:
        pl.loop(0, blocks)(first_layer)
    og_onward()

    for copy in nb_copies:
        copy.wait()
    for at in range(0, nb_all.shape[0], 128):
        turned = jnp.transpose(nb_all[at : at + 128, :])
        for j in range(min(16, n - at // 8)):
            t = at // 8 + j
            nb_nat[t * own : (t + 1) * own, :8] = turned[:own, j * 8 : j * 8 + 8]
    counts_matrix(nb_nat, 0, smat, 0, targets, full)
    picks_t[...] = jnp.transpose(picks[...])
    for lane, size in split(full, 128):
        smat_t[lane : lane + size, :] = jnp.transpose(smat[:, lane : lane + size])

    value = part32[mine, :] + b1[...]
    for i in range(1, n):
        source = lax.rem(f + i, n)
        pltpu.make_async_remote_copy(
            part16.at[pl.ds(0, own)], rs_buf.at[source], rs_s.at[source], rs_r.at[source],
            device_id={"feat": source}, device_id_type=MESH,
        ).wait_recv()
        value = value + rs_buf[source].astype(F32)
    pre_own[...] = value.astype(BF16)
    pre_all[mine, :] = value.astype(BF16)
    onward, finish = gather(pre_own, pre_all, ag_s, ag_r)
    for copy in late:
        copy.wait()
    og_finish()

    def out_part(i):
        rows = pl.ds(pl.multiple_of(i * block, block), block)
        grad_act[rows if blocks <= 2 else slice(None), :] = dot_last(og_all[rows, :], wout[...])

    if blocks <= 2:
        steps(blocks, out_part)

    onward()
    early = (len(cols) + 1) // 2
    for lane, size in cols[:early]:
        agg_t[lane : lane + size, :] = jnp.transpose(agg[:, lane : lane + size])
    finish()

    def hidden_part(i):
        rows = pl.ds(pl.multiple_of(i * block, block), block)
        value = pre_all[rows, :].astype(F32)
        ext[rows, :] = (value * sigmoid(value)).astype(BF16)

    steps(blocks, hidden_part)
    halo_out[...] = dot(picks_t[...], ext[:targets, :]).astype(BF16)
    halo_copy = pltpu.make_async_remote_copy(
        halo_out, ext.at[pl.ds(targets, halo)], halo_sem.at[0], halo_sem.at[1],
        device_id={"dp": lax.rem(d + 1, parts)}, device_id_type=MESH,
    )
    halo_copy.start()

    def neighbour_part(i):
        rows = pl.ds(pl.multiple_of(i * block, block), block)
        gagg[rows, :] = dot(smat[rows, :targets], ext[:targets, :])

    steps(blocks, neighbour_part)
    for lane, size in cols[early:]:
        agg_t[lane : lane + size, :] = jnp.transpose(agg[:, lane : lane + size])
    halo_copy.wait()

    def second_layer(i):
        rows = pl.ds(pl.multiple_of(i * block, block), block)
        inv = inverse(nb_nat[rows, :8])
        if blocks > 2:
            out_part(i)
        total = gagg[rows, :] + dot(smat[rows, targets:], ext[targets:, :])
        value = (ext[rows, :].astype(F32) + total * inv).astype(BF16)
        agg2[rows, :] = value
        step = (grad_act[rows if blocks <= 2 else slice(None), :] * slope(dot(value, win[...]))).astype(BF16)
        back = dot_last(step, win[...])
        gagg[rows, :] = back
        gscaled[rows, :] = (back * inv).astype(BF16)

    steps(blocks, second_layer)

    back_out[...] = dot(smat_t[targets:, :], gscaled[...]).astype(BF16)
    back_copy = pltpu.make_async_remote_copy(
        back_out, back_in, back_sem.at[0], back_sem.at[1],
        device_id={"dp": lax.rem(d + parts - 1, parts)}, device_id_type=MESH,
    )
    back_copy.start()

    for at, size in split(targets, 512):
        rows = slice(at, at + size)
        gtotal[rows, :] = (
            og_all[rows, :].astype(F32) + gagg[rows, :] + dot(smat_t[rows, :], gscaled[...])
        )
    value = dot(agg2[mine, :], win[...])
    act = (value * sigmoid(value)).astype(BF16)
    embed[...] = (ext[mine, :].astype(F32) + dot(act, wout[...])).astype(BF16)

    back_copy.wait()

    def first_gradient(i):
        rows = pl.ds(pl.multiple_of(i * block, block), block)
        value = gtotal[rows, :] + dot(picks[rows, :], back_in[...])
        gp[rows, :] = (value * slope(pre_all[rows, :].astype(F32))).astype(BF16)

    steps(blocks, first_gradient)

    half = width // 2
    size = half // chunks
    side = lax.rem(d, 2)
    chip = d // 2
    chips = parts // 2
    mate = d + 1 - 2 * side

    def place(which, c):
        return pl.ds(pl.multiple_of(which * half + c * size, 16), size)

    pair_copies, chip_copies, end_copies = [], [], []
    for c in range(chunks):
        span = slice(c * size, (c + 1) * size)
        pair_out[span, :] = dot(agg_t[place(1 - side, c), :], gp[...]).astype(BF16)
        copy = pltpu.make_async_remote_copy(
            pair_out.at[pl.ds(c * size, size)], pair_in.at[pl.ds(c * size, size)], pa_s.at[c], pa_r.at[c],
            device_id={"dp": mate}, device_id_type=MESH,
        )
        copy.start()
        pair_copies.append(copy)
    for c in range(chunks):
        span = slice(c * size, (c + 1) * size)
        value = dot(agg_t[place(side, c), :], gp[...])
        pair_copies[c].wait()
        chip_buf[chip, span, :] = (value + pair_in[span, :].astype(F32)).astype(BF16)
        for i in range(1, chips):
            here = chip_buf.at[chip, pl.ds(c * size, size)]
            copy = pltpu.make_async_remote_copy(
                here, here, x_s.at[i, c], x_r.at[i, c],
                device_id={"dp": lax.rem(d + 2 * i, parts)}, device_id_type=MESH,
            )
            copy.start()
            chip_copies.append(copy)
    for c in range(chunks):
        span = slice(c * size, (c + 1) * size)
        for copy in chip_copies[c * (chips - 1) : (c + 1) * (chips - 1)]:
            copy.wait()
        total = chip_buf[0, span, :].astype(F32)
        for i in range(1, chips):
            total = total + chip_buf[i, span, :].astype(F32)
        grad[place(side, c), :] = total.astype(BF16)
        there = grad.at[place(side, c)]
        copy = pltpu.make_async_remote_copy(
            there, there, pb_s.at[c], pb_r.at[c], device_id={"dp": mate}, device_id_type=MESH,
        )
        copy.start()
        end_copies.append(copy)
    for copy in end_copies:
        copy.wait()
    for i in range(1, n):
        send_to(lax.rem(f + i, n)).wait_send()


def finish_kernel(embed_in, grad_in, embed, grad, narrow, wide, in_sem, out_sem):
    rows, pieces = grad_in.shape[0], in_sem.shape[0] - 1
    size = rows // pieces
    small = pltpu.make_async_copy(embed_in, embed, in_sem.at[pieces])
    small.start()

    def part(ref, i):
        return ref.at[pl.ds(i * size, size)]

    arrive = [
        pltpu.make_async_copy(part(grad_in, i), part(narrow, i), in_sem.at[i]) for i in range(pieces)
    ]
    leave = [pltpu.make_async_copy(part(wide, i), part(grad, i), out_sem.at[i]) for i in range(pieces)]
    for copy in arrive:
        copy.start()
    for i in range(pieces):
        arrive[i].wait()
        span = slice(i * size, (i + 1) * size)
        wide[span, :] = narrow[span, :].astype(F32)
        leave[i].start()
    small.wait()
    for copy in leave:
        copy.wait()


def finished(embed, grad):
    pieces = next(c for c in (4, 2, 1) if (grad.shape[0] // c) % 16 == 0)
    any_space = pl.BlockSpec(memory_space=pl.ANY)
    return pl.pallas_call(
        finish_kernel,
        out_shape=(
            jax.ShapeDtypeStruct(embed.shape, BF16),
            jax.ShapeDtypeStruct(grad.shape, F32),
        ),
        in_specs=[any_space, any_space],
        out_specs=(any_space, any_space),
        scratch_shapes=[
            pltpu.VMEM(grad.shape, BF16),
            pltpu.VMEM(grad.shape, F32),
            pltpu.SemaphoreType.DMA((pieces + 1,)),
            pltpu.SemaphoreType.DMA((pieces,)),
        ],
        compiler_params=pltpu.CompilerParams(vmem_limit_bytes=56 * 1024 * 1024),
        name="finish",
    )(embed, grad)


def fused(
    n, parts, face_grid, nb1, count1, w_first, b_first, send_rows, nb2, count2, w_in, w_out, out_grad
):
    src, width = face_grid.shape
    targets, hid = nb1.shape[1], w_first.shape[1]
    inner = w_in.shape[1]
    own, halo = nb2.shape[1], send_rows.shape[1]
    full = targets + halo
    block = min(targets, 256)
    half = width // 2
    chunks = next(c for c in (4, 2, 1) if (half // c) % 16 == 0)
    chips = parts // 2
    tiles = -(-n * 8 // 128) * 128
    any_space = pl.BlockSpec(memory_space=pl.ANY)
    vmem = pl.BlockSpec(memory_space=pltpu.VMEM)
    dma = pltpu.SemaphoreType.DMA
    return pl.pallas_call(
        functools.partial(kernel, n, parts, block, chunks),
        out_shape=(
            jax.ShapeDtypeStruct((own, hid), BF16),
            jax.ShapeDtypeStruct((width, hid), BF16),
        ),
        in_specs=[
            any_space, vmem, vmem, any_space, vmem, vmem, vmem, vmem, any_space, any_space, vmem,
        ],
        out_specs=(vmem, vmem),
        scratch_shapes=[
            pltpu.VMEM((src, width), BF16),
            pltpu.VMEM((width, hid), BF16),
            pltpu.VMEM((hid, inner), BF16),
            pltpu.VMEM((inner, hid), BF16),
            pltpu.VMEM((block, src), BF16),
            pltpu.VMEM((targets, width), BF16),
            pltpu.VMEM((width, targets), BF16),
            pltpu.VMEM((targets, hid), F32),
            pltpu.VMEM((targets, hid), BF16),
            pltpu.VMEM((n, own, hid), BF16),
            pltpu.VMEM((own, hid), BF16),
            pltpu.VMEM((targets, hid), BF16),
            pltpu.VMEM((full, hid), BF16),
            pltpu.VMEM((targets, halo), BF16),
            pltpu.VMEM((halo, targets), BF16),
            pltpu.VMEM((targets, hid), BF16),
            pltpu.VMEM((targets, 128), F32),
            pltpu.VMEM((8, 128), F32),
            pltpu.VMEM((tiles, 128), F32),
            pltpu.VMEM((targets, 128), F32),
            pltpu.VMEM((targets, full), BF16),
            pltpu.VMEM((full, targets), BF16),
            pltpu.VMEM((targets if targets // block <= 2 else block, inner), F32),
            pltpu.VMEM((targets, hid), BF16),
            pltpu.VMEM((targets, hid), BF16),
            pltpu.VMEM((targets, hid), F32),
            pltpu.VMEM((halo, hid), BF16),
            pltpu.VMEM((halo, hid), BF16),
            pltpu.VMEM((halo, hid), BF16),
            pltpu.VMEM((targets, hid), F32),
            pltpu.VMEM((targets, hid), BF16),
            pltpu.VMEM((half, hid), BF16),
            pltpu.VMEM((half, hid), BF16),
            pltpu.VMEM((chips, half, hid), BF16),
            dma((len(split(width, 256)) + 3,)),
            dma((n,)), dma((n,)),
            dma((2, n // 2)), dma((2, n // 2)), dma((2, n // 2)), dma((2, n // 2)),
            dma((n,)), dma((n,)),
            dma((2,)), dma((2,)),
            dma((chunks,)), dma((chunks,)),
            dma((chips, chunks)), dma((chips, chunks)),
            dma((chunks,)), dma((chunks,)),
        ],
        compiler_params=pltpu.CompilerParams(
            collective_id=0, has_side_effects=True, vmem_limit_bytes=60 * 1024 * 1024
        ),
        cost_estimate=pl.CostEstimate(
            flops=2 * targets * src * width, bytes_accessed=2 * src * width, transcendentals=0
        ),
        name="fused_step",
    )(
        face_grid, nb1, count1, w_first, b_first, send_rows, nb2, count2, w_in, w_out, out_grad
    )


def solution(mesh):
    n, parts = mesh.shape["feat"], mesh.shape["dp"]

    def body(
        face_grid, first_nbrs, first_count, w_first, b_first, send_rows,
        second_nbrs, second_count, w_in, w_out, out_grad,
    ):
        embed, grad = fused(
            n, parts, face_grid, first_nbrs.T, first_count.reshape(1, -1), w_first,
            b_first.reshape(1, -1), send_rows.reshape(1, -1), second_nbrs.T,
            second_count.reshape(1, -1), w_in, w_out, out_grad,
        )
        return finished(embed, grad)

    return jax.shard_map(
        body,
        mesh=mesh,
        in_specs=(
            P("dp", "feat"), P("dp", None), P("dp"), P("feat", None), P(), P("dp"),
            P(("dp", "feat"), None), P(("dp", "feat")), P(), P(), P(("dp", "feat"), None),
        ),
        out_specs=(P(("dp", "feat"), None), P("feat", None)),
        check_vma=False,
    )
```

```python
import functools

import jax
import jax.numpy as jnp
from jax import lax
from jax.experimental import pallas as pl
from jax.experimental.pallas import tpu as pltpu
from jax.sharding import PartitionSpec as P

MESH = pl.DeviceIdType.MESH
F32, BF16 = jnp.float32, jnp.bfloat16


def dot(a, b):
    return jnp.dot(a, b, preferred_element_type=F32)


def dot_last(a, b):
    return lax.dot_general(a, b, (((1,), (1,)), ((), ())), preferred_element_type=F32)


def sigmoid(value):
    return 0.5 * jnp.tanh(0.5 * value) + 0.5


def slope(value):
    sig = sigmoid(value)
    return sig * (1.0 + value * (1.0 - sig))


def steps(count, fn):
    if count <= 1:
        for i in range(count):
            fn(i)
    else:
        pl.loop(0, count)(fn)


def split(size, width):
    return [(at, min(width, size - at)) for at in range(0, size, width)]


def counts_matrix(nbrs, source, out, at, rows, width):
    spots = [
        (lane, size, (lax.broadcasted_iota(jnp.int32, (8, size), 1) + lane).astype(F32))
        for lane, size in split(width, 1024)
    ]

    def group(g):
        for lane, size, spot in spots:
            pieces = []
            for piece in range(2):
                names = nbrs[pl.ds(pl.multiple_of(source + g * 16 + piece * 8, 8), 8), :8]
                total = jnp.zeros((8, size), F32)
                for slot in range(8):
                    total = total + jnp.where(names[:, slot : slot + 1] == spot, 1.0, 0.0)
                pieces.append(total)
            here = pl.ds(pl.multiple_of(at + g * 16, 16), 16)
            out[here, lane : lane + size] = jnp.concatenate(pieces, axis=0).astype(BF16)

    several = 4 if width <= 1024 and rows % 64 == 0 else 1

    def groups(i):
        for j in range(several):
            group(i * several + j)

    pl.loop(0, rows // 16 // several)(groups)


def live(nbrs, count):
    slots = lax.broadcasted_iota(jnp.int32, nbrs.shape, 0)
    return jnp.where(slots < count, nbrs, -1).astype(F32)


def inverse(names):
    live = jnp.where(names >= 0, 1.0, 0.0)
    return 1.0 / jnp.sum(live, axis=1, keepdims=True)


def kernel(
    n, parts, block, chunks,
    face_hbm, nb1_t, count1, w1_hbm, b1, srows, nb2_t, count2, win_hbm, wout_hbm, og,
    embed, grad,
    face, w1, win, wout, adj, agg, agg_t, part32, part16, pair_buf, sums, pre_sum, rs_buf, pre_own, pre_all,
    ext, picks, picks_t, og_all, nb1, nb_send, nb_all, nb_nat, smat, smat_t, grad_act, agg2, gscaled, gagg,
    halo_out, back_out, back_in, gtotal, gp, pair_out, pair_in, chip_buf,
    load_sem, pr_s, pr_r, rs_s, rs_r, ag_s, ag_r, og_s, og_r, nb_s, nb_r, halo_sem, back_sem,
    pa_s, pa_r, x_s, x_r, pb_s, pb_r,
):
    f, d = lax.axis_index("feat"), lax.axis_index("dp")
    src, width = face.shape
    targets, hid = nb1.shape[0], w1.shape[1]
    own = og.shape[0]
    halo = srows.shape[1]
    full = targets + halo
    mine = pl.ds(pl.multiple_of(f * own, own), own)
    cols = split(width, 256)

    loads = [
        pltpu.make_async_copy(face_hbm.at[:, pl.ds(at, size)], face.at[:, pl.ds(at, size)], load_sem.at[i])
        for i, (at, size) in enumerate(cols)
    ]
    loads.append(pltpu.make_async_copy(w1_hbm, w1, load_sem.at[len(cols)]))
    late = [
        pltpu.make_async_copy(wout_hbm, wout, load_sem.at[len(cols) + 1]),
        pltpu.make_async_copy(win_hbm, win, load_sem.at[len(cols) + 2]),
    ]
    for copy in loads + late:
        copy.start()

    barrier = pltpu.get_barrier_semaphore()
    for i in range(1, n):
        pl.semaphore_signal(barrier, inc=1, device_id={"feat": lax.rem(f + i, n)}, device_id_type=MESH)
    for i in range(1, parts):
        pl.semaphore_signal(barrier, inc=1, device_id={"dp": lax.rem(d + i, parts)}, device_id_type=MESH)

    nb_send[...] = jnp.full(nb_send.shape, -1.0, F32)
    nb_send[:, :own] = live(nb2_t[...], count2[...])
    if nb_all.shape[0] > n * 8:
        nb_all[n * 8 :, :] = jnp.full((nb_all.shape[0] - n * 8, 128), -1.0, F32)
    nb_all[pl.ds(pl.multiple_of(f * 8, 8), 8), :] = nb_send[...]
    og_all[mine, :] = og[...]
    picks[...] = jnp.where(
        lax.broadcasted_iota(jnp.int32, (targets, halo), 0) == srows[...], 1.0, 0.0
    ).astype(BF16)
    names = live(nb1_t[...], count1[...])
    for at in range(0, targets, 128):
        tile = jnp.concatenate([names[:, at : at + 128], jnp.zeros((120, 128), F32)], axis=0)
        nb1[at : at + 128, :] = jnp.transpose(tile)

    blocks = targets // block
    per = block // own
    first = lax.rem(f // per + 1, blocks)
    counts_matrix(nb1, pl.multiple_of(first * block, block), adj, 0, block, src)

    pl.semaphore_wait(barrier, n - 1 + parts - 1)

    pair = f + 1 - 2 * lax.rem(f, 2)
    outer = n // 2

    def held(buffer, owner):
        return buffer.at[pl.ds(pl.multiple_of(owner * own, own), own)]

    def gather(source, buffer, sends, recvs):
        first_hop = [
            pltpu.make_async_remote_copy(
                source, held(buffer, f), sends.at[0, i], recvs.at[0, i],
                device_id={"feat": lax.rem(f + 2 * i, n)}, device_id_type=MESH,
            )
            for i in range(1, outer)
        ]
        to_mate = [
            pltpu.make_async_remote_copy(
                source, held(buffer, f), sends.at[1, 0], recvs.at[1, 0],
                device_id={"feat": pair}, device_id_type=MESH,
            )
        ]
        for copy in first_hop + to_mate:
            copy.start()

        def onward():
            for i in range(1, outer):
                first_hop[i - 1].wait_recv()
                owner = held(buffer, lax.rem(f + n - 2 * i, n))
                copy = pltpu.make_async_remote_copy(
                    owner, owner, sends.at[1, i], recvs.at[1, i],
                    device_id={"feat": pair}, device_id_type=MESH,
                )
                copy.start()
                to_mate.append(copy)

        def finish():
            for copy in first_hop:
                copy.wait_send()
            for copy in to_mate:
                copy.wait()

        return onward, finish

    nb_copies = []
    for i in range(1, n):
        copy = pltpu.make_async_remote_copy(
            nb_send, nb_all.at[pl.ds(pl.multiple_of(f * 8, 8), 8)], nb_s.at[i], nb_r.at[i],
            device_id={"feat": lax.rem(f + i, n)}, device_id_type=MESH,
        )
        copy.start()
        nb_copies.append(copy)
    og_onward, og_finish = gather(og, og_all, og_s, og_r)

    column, parity = f // 2, lax.rem(f, 2)

    def to_pair(other):
        there = pl.ds(pl.multiple_of((2 * other + 1 - parity) * own, own), own)
        return pltpu.make_async_remote_copy(
            part16.at[there], pair_buf.at[other], pr_s.at[other], pr_r.at[other],
            device_id={"feat": pair}, device_id_type=MESH,
        )

    def to_owner(other):
        return pltpu.make_async_remote_copy(
            sums.at[other], rs_buf.at[column], rs_s.at[other], rs_r.at[column],
            device_id={"feat": 2 * other + parity}, device_id_type=MESH,
        )

    def by_columns(fn, first_col, last_col):
        if width % 256 == 0:
            pl.loop(first_col, last_col)(lambda j: fn(pl.multiple_of(j * 256, 256), 256))
        else:
            for lane, size in cols[first_col:last_col]:
                fn(lane, size)

    for copy in loads:
        copy.wait()

    def first_layer(i):
        which = lax.rem(first + i, blocks)
        at = pl.multiple_of(which * block, block)
        rows = pl.ds(at, block)
        if blocks > 1:
            pl.when(i > 0)(lambda: counts_matrix(nb1, at, adj, 0, block, src))
        inv = inverse(nb1[rows, :8])
        part32[rows, :] = jnp.zeros((block, hid), F32)

        def column_part(lane, size):
            chunk = pl.ds(lane, size)
            value = dot(adj[...], face[:, chunk]) * inv + face[rows, chunk].astype(F32)
            value = value.astype(BF16)
            agg[rows, chunk] = value
            part32[rows, :] += dot(value, w1[chunk, :])

        by_columns(column_part, 0, len(cols))
        part16[rows, :] = part32[rows, :].astype(BF16)
        for j in range(per // 2):
            to_pair(which * (per // 2) + j).start()

    steps(blocks, first_layer)

    side_size = outer // 2
    side_at = column // side_size * side_size
    far_at = (outer - side_size) - side_at
    far = [far_at + lax.rem(column + i, side_size) for i in range(side_size)]
    near = [side_at + lax.rem(column + i, side_size) for i in range(1, side_size)]

    def pair_sum(other):
        to_pair(other).wait_recv()
        rows = pl.ds(pl.multiple_of((2 * other + parity) * own, own), own)
        return part32[rows, :] + pair_buf[other].astype(F32)

    for other in far + near:
        sums[other] = pair_sum(other).astype(BF16)
        to_owner(other).start()
    pre_sum[...] = pair_sum(column) + b1[...]
    og_onward()

    for copy in nb_copies:
        copy.wait()
    for at in range(0, nb_all.shape[0], 128):
        turned = jnp.transpose(nb_all[at : at + 128, :])
        for j in range(min(16, n - at // 8)):
            t = at // 8 + j
            nb_nat[t * own : (t + 1) * own, :8] = turned[:own, j * 8 : j * 8 + 8]
    counts_matrix(nb_nat, 0, smat, 0, targets, full)
    picks_t[...] = jnp.transpose(picks[...])

    def turn_smat(j):
        lane = pl.ds(pl.multiple_of(j * 128, 128), 128)
        smat_t[lane, :] = jnp.transpose(smat[:, lane])

    pl.loop(0, full // 128)(turn_smat)

    value = pre_sum[...]
    for other in far + near:
        pltpu.make_async_remote_copy(
            sums.at[other], rs_buf.at[other], rs_s.at[other], rs_r.at[other],
            device_id={"feat": 2 * other + parity}, device_id_type=MESH,
        ).wait_recv()
        value = value + rs_buf[other].astype(F32)
    pre_own[...] = value.astype(BF16)
    pre_all[mine, :] = value.astype(BF16)
    onward, finish = gather(pre_own, pre_all, ag_s, ag_r)
    for copy in late:
        copy.wait()
    og_finish()

    def out_part(i):
        rows = pl.ds(pl.multiple_of(i * block, block), block)
        grad_act[rows if blocks <= 2 else slice(None), :] = dot_last(og_all[rows, :], wout[...])

    if blocks <= 2:
        steps(blocks, out_part)

    onward()
    early = (len(cols) + 1) // 2

    def turn_agg(lane, size):
        agg_t[pl.ds(lane, size), :] = jnp.transpose(agg[:, pl.ds(lane, size)])

    by_columns(turn_agg, 0, early)
    finish()

    def hidden_part(i):
        rows = pl.ds(pl.multiple_of(i * block, block), block)
        value = pre_all[rows, :].astype(F32)
        ext[rows, :] = (value * sigmoid(value)).astype(BF16)

    steps(blocks, hidden_part)
    halo_out[...] = dot(picks_t[...], ext[:targets, :]).astype(BF16)
    halo_copy = pltpu.make_async_remote_copy(
        halo_out, ext.at[pl.ds(targets, halo)], halo_sem.at[0], halo_sem.at[1],
        device_id={"dp": lax.rem(d + 1, parts)}, device_id_type=MESH,
    )
    halo_copy.start()

    def neighbour_part(i):
        rows = pl.ds(pl.multiple_of(i * block, block), block)
        gagg[rows, :] = dot(smat[rows, :targets], ext[:targets, :])

    steps(blocks, neighbour_part)
    by_columns(turn_agg, early, len(cols))
    halo_copy.wait()

    def second_layer(i):
        rows = pl.ds(pl.multiple_of(i * block, block), block)
        inv = inverse(nb_nat[rows, :8])
        if blocks > 2:
            out_part(i)
        total = gagg[rows, :] + dot(smat[rows, targets:], ext[targets:, :])
        value = (ext[rows, :].astype(F32) + total * inv).astype(BF16)
        agg2[rows, :] = value
        step = (grad_act[rows if blocks <= 2 else slice(None), :] * slope(dot(value, win[...]))).astype(BF16)
        back = dot_last(step, win[...])
        gagg[rows, :] = back
        gscaled[rows, :] = (back * inv).astype(BF16)

    steps(blocks, second_layer)

    back_out[...] = dot(smat_t[targets:, :], gscaled[...]).astype(BF16)
    back_copy = pltpu.make_async_remote_copy(
        back_out, back_in, back_sem.at[0], back_sem.at[1],
        device_id={"dp": lax.rem(d + parts - 1, parts)}, device_id_type=MESH,
    )
    back_copy.start()

    for at, size in split(targets, 512):
        rows = slice(at, at + size)
        gtotal[rows, :] = (
            og_all[rows, :].astype(F32) + gagg[rows, :] + dot(smat_t[rows, :], gscaled[...])
        )
    value = dot(agg2[mine, :], win[...])
    act = (value * sigmoid(value)).astype(BF16)
    embed[...] = (ext[mine, :].astype(F32) + dot(act, wout[...])).astype(BF16)

    back_copy.wait()

    def first_gradient(i):
        rows = pl.ds(pl.multiple_of(i * block, block), block)
        value = gtotal[rows, :] + dot(picks[rows, :], back_in[...])
        gp[rows, :] = (value * slope(pre_all[rows, :].astype(F32))).astype(BF16)

    steps(blocks, first_gradient)

    half = width // 2
    size = half // chunks
    side = lax.rem(d, 2)
    chip = d // 2
    chips = parts // 2
    mate = d + 1 - 2 * side

    def place(which, c):
        return pl.ds(pl.multiple_of(which * half + c * size, 16), size)

    pair_copies, chip_copies, end_copies = [], [], []
    for c in range(chunks):
        span = slice(c * size, (c + 1) * size)
        pair_out[span, :] = dot(agg_t[place(1 - side, c), :], gp[...]).astype(BF16)
        copy = pltpu.make_async_remote_copy(
            pair_out.at[pl.ds(c * size, size)], pair_in.at[pl.ds(c * size, size)], pa_s.at[c], pa_r.at[c],
            device_id={"dp": mate}, device_id_type=MESH,
        )
        copy.start()
        pair_copies.append(copy)
    for c in range(chunks):
        span = slice(c * size, (c + 1) * size)
        value = dot(agg_t[place(side, c), :], gp[...])
        pair_copies[c].wait()
        chip_buf[chip, span, :] = (value + pair_in[span, :].astype(F32)).astype(BF16)
        for i in range(1, chips):
            here = chip_buf.at[chip, pl.ds(c * size, size)]
            copy = pltpu.make_async_remote_copy(
                here, here, x_s.at[i, c], x_r.at[i, c],
                device_id={"dp": lax.rem(d + 2 * i, parts)}, device_id_type=MESH,
            )
            copy.start()
            chip_copies.append(copy)
    for c in range(chunks):
        span = slice(c * size, (c + 1) * size)
        for copy in chip_copies[c * (chips - 1) : (c + 1) * (chips - 1)]:
            copy.wait()
        total = chip_buf[0, span, :].astype(F32)
        for i in range(1, chips):
            total = total + chip_buf[i, span, :].astype(F32)
        grad[place(side, c), :] = total.astype(BF16)
        there = grad.at[place(side, c)]
        copy = pltpu.make_async_remote_copy(
            there, there, pb_s.at[c], pb_r.at[c], device_id={"dp": mate}, device_id_type=MESH,
        )
        copy.start()
        end_copies.append(copy)
    for copy in end_copies:
        copy.wait()
    for other in range(outer):
        to_pair(other).wait_send()
    for other in far + near:
        to_owner(other).wait_send()


def finish_kernel(embed_in, grad_in, embed, grad, narrow, wide, in_sem, out_sem):
    rows, pieces = grad_in.shape[0], in_sem.shape[0] - 1
    size = rows // pieces
    small = pltpu.make_async_copy(embed_in, embed, in_sem.at[pieces])
    small.start()

    def part(ref, i):
        return ref.at[pl.ds(i * size, size)]

    arrive = [
        pltpu.make_async_copy(part(grad_in, i), part(narrow, i), in_sem.at[i]) for i in range(pieces)
    ]
    leave = [pltpu.make_async_copy(part(wide, i), part(grad, i), out_sem.at[i]) for i in range(pieces)]
    for copy in arrive:
        copy.start()
    for i in range(pieces):
        arrive[i].wait()
        span = slice(i * size, (i + 1) * size)
        wide[span, :] = narrow[span, :].astype(F32)
        leave[i].start()
    small.wait()
    for copy in leave:
        copy.wait()


def finished(embed, grad):
    pieces = next(c for c in (4, 2, 1) if (grad.shape[0] // c) % 16 == 0)
    any_space = pl.BlockSpec(memory_space=pl.ANY)
    return pl.pallas_call(
        finish_kernel,
        out_shape=(
            jax.ShapeDtypeStruct(embed.shape, BF16),
            jax.ShapeDtypeStruct(grad.shape, F32),
        ),
        in_specs=[any_space, any_space],
        out_specs=(any_space, any_space),
        scratch_shapes=[
            pltpu.VMEM(grad.shape, BF16),
            pltpu.VMEM(grad.shape, F32),
            pltpu.SemaphoreType.DMA((pieces + 1,)),
            pltpu.SemaphoreType.DMA((pieces,)),
        ],
        compiler_params=pltpu.CompilerParams(vmem_limit_bytes=56 * 1024 * 1024),
        name="finish",
    )(embed, grad)


def fused(
    n, parts, face_grid, nb1, count1, w_first, b_first, send_rows, nb2, count2, w_in, w_out, out_grad
):
    src, width = face_grid.shape
    targets, hid = nb1.shape[1], w_first.shape[1]
    inner = w_in.shape[1]
    own, halo = nb2.shape[1], send_rows.shape[1]
    full = targets + halo
    block = min(targets, 256)
    half = width // 2
    chunks = next(c for c in (4, 2, 1) if (half // c) % 16 == 0)
    chips = parts // 2
    tiles = -(-n * 8 // 128) * 128
    any_space = pl.BlockSpec(memory_space=pl.ANY)
    vmem = pl.BlockSpec(memory_space=pltpu.VMEM)
    dma = pltpu.SemaphoreType.DMA
    return pl.pallas_call(
        functools.partial(kernel, n, parts, block, chunks),
        out_shape=(
            jax.ShapeDtypeStruct((own, hid), BF16),
            jax.ShapeDtypeStruct((width, hid), BF16),
        ),
        in_specs=[
            any_space, vmem, vmem, any_space, vmem, vmem, vmem, vmem, any_space, any_space, vmem,
        ],
        out_specs=(vmem, vmem),
        scratch_shapes=[
            pltpu.VMEM((src, width), BF16),
            pltpu.VMEM((width, hid), BF16),
            pltpu.VMEM((hid, inner), BF16),
            pltpu.VMEM((inner, hid), BF16),
            pltpu.VMEM((block, src), BF16),
            pltpu.VMEM((targets, width), BF16),
            pltpu.VMEM((width, targets), BF16),
            pltpu.VMEM((targets, hid), F32),
            pltpu.VMEM((targets, hid), BF16),
            pltpu.VMEM((n // 2, own, hid), BF16),
            pltpu.VMEM((n // 2, own, hid), BF16),
            pltpu.VMEM((own, hid), F32),
            pltpu.VMEM((n // 2, own, hid), BF16),
            pltpu.VMEM((own, hid), BF16),
            pltpu.VMEM((targets, hid), BF16),
            pltpu.VMEM((full, hid), BF16),
            pltpu.VMEM((targets, halo), BF16),
            pltpu.VMEM((halo, targets), BF16),
            pltpu.VMEM((targets, hid), BF16),
            pltpu.VMEM((targets, 128), F32),
            pltpu.VMEM((8, 128), F32),
            pltpu.VMEM((tiles, 128), F32),
            pltpu.VMEM((targets, 128), F32),
            pltpu.VMEM((targets, full), BF16),
            pltpu.VMEM((full, targets), BF16),
            pltpu.VMEM((targets if targets // block <= 2 else block, inner), F32),
            pltpu.VMEM((targets, hid), BF16),
            pltpu.VMEM((targets, hid), BF16),
            pltpu.VMEM((targets, hid), F32),
            pltpu.VMEM((halo, hid), BF16),
            pltpu.VMEM((halo, hid), BF16),
            pltpu.VMEM((halo, hid), BF16),
            pltpu.VMEM((targets, hid), F32),
            pltpu.VMEM((targets, hid), BF16),
            pltpu.VMEM((half, hid), BF16),
            pltpu.VMEM((half, hid), BF16),
            pltpu.VMEM((chips, half, hid), BF16),
            dma((len(split(width, 256)) + 3,)),
            dma((n // 2,)), dma((n // 2,)), dma((n // 2,)), dma((n // 2,)),
            dma((2, n // 2)), dma((2, n // 2)), dma((2, n // 2)), dma((2, n // 2)),
            dma((n,)), dma((n,)),
            dma((2,)), dma((2,)),
            dma((chunks,)), dma((chunks,)),
            dma((chips, chunks)), dma((chips, chunks)),
            dma((chunks,)), dma((chunks,)),
        ],
        compiler_params=pltpu.CompilerParams(
            collective_id=0, has_side_effects=True, vmem_limit_bytes=60 * 1024 * 1024
        ),
        cost_estimate=pl.CostEstimate(
            flops=2 * targets * src * width, bytes_accessed=2 * src * width, transcendentals=0
        ),
        name="fused_step",
    )(
        face_grid, nb1, count1, w_first, b_first, send_rows, nb2, count2, w_in, w_out, out_grad
    )


def solution(mesh):
    n, parts = mesh.shape["feat"], mesh.shape["dp"]

    def body(
        face_grid, first_nbrs, first_count, w_first, b_first, send_rows,
        second_nbrs, second_count, w_in, w_out, out_grad,
    ):
        embed, grad = fused(
            n, parts, face_grid, first_nbrs.T, first_count.reshape(1, -1), w_first,
            b_first.reshape(1, -1), send_rows.reshape(1, -1), second_nbrs.T,
            second_count.reshape(1, -1), w_in, w_out, out_grad,
        )
        return finished(embed, grad)

    return jax.shard_map(
        body,
        mesh=mesh,
        in_specs=(
            P("dp", "feat"), P("dp", None), P("dp"), P("feat", None), P(), P("dp"),
            P(("dp", "feat"), None), P(("dp", "feat")), P(), P(), P(("dp", "feat"), None),
        ),
        out_specs=(P(("dp", "feat"), None), P("feat", None)),
        check_vma=False,
    )
```

```python
import functools

import jax
import jax.numpy as jnp
from jax import lax
from jax.experimental import pallas as pl
from jax.experimental.pallas import tpu as pltpu
from jax.sharding import PartitionSpec as P

MESH = pl.DeviceIdType.MESH
F32, BF16 = jnp.float32, jnp.bfloat16


def dot(a, b):
    return jnp.dot(a, b, preferred_element_type=F32)


def dot_last(a, b):
    return lax.dot_general(a, b, (((1,), (1,)), ((), ())), preferred_element_type=F32)


def sigmoid(value):
    return 0.5 * jnp.tanh(0.5 * value) + 0.5


def slope(value):
    sig = sigmoid(value)
    return sig * (1.0 + value * (1.0 - sig))


def steps(count, fn):
    if count <= 1:
        for i in range(count):
            fn(i)
    else:
        pl.loop(0, count)(fn)


def split(size, width):
    return [(at, min(width, size - at)) for at in range(0, size, width)]


def counts_matrix(nbrs, source, out, at, rows, width):
    spots = [
        (lane, size, (lax.broadcasted_iota(jnp.int32, (8, size), 1) + lane).astype(F32))
        for lane, size in split(width, 1024)
    ]

    def group(g):
        for lane, size, spot in spots:
            pieces = []
            for piece in range(2):
                names = nbrs[pl.ds(pl.multiple_of(source + g * 16 + piece * 8, 8), 8), :8]
                total = jnp.zeros((8, size), F32)
                for slot in range(8):
                    total = total + jnp.where(names[:, slot : slot + 1] == spot, 1.0, 0.0)
                pieces.append(total)
            here = pl.ds(pl.multiple_of(at + g * 16, 16), 16)
            out[here, lane : lane + size] = jnp.concatenate(pieces, axis=0).astype(BF16)

    several = 4 if width <= 1024 and rows % 64 == 0 else 1

    def groups(i):
        for j in range(several):
            group(i * several + j)

    pl.loop(0, rows // 16 // several)(groups)


def live(nbrs, count):
    slots = lax.broadcasted_iota(jnp.int32, nbrs.shape, 0)
    return jnp.where(slots < count, nbrs, -1).astype(F32)


def inverse(names):
    live = jnp.where(names >= 0, 1.0, 0.0)
    return 1.0 / jnp.sum(live, axis=1, keepdims=True)


def kernel(
    n, parts, block, chunks,
    face_hbm, nb1_t, count1, w1_hbm, b1, srows, nb2_t, count2, win_hbm, wout_hbm, og,
    embed, grad,
    face, w1, win, wout, adj, agg, agg_t, part32, part16, pair_buf, sums, pre_sum, rs_buf, pre_own, pre_all,
    ext, picks, picks_t, og_all, nb1, nb_send, nb_all, nb_nat, smat, smat_t, grad_act, agg2, gscaled, gagg,
    halo_out, back_out, back_in, gtotal, gp, pair_out, pair_in, chip_buf, eye,
    load_sem, pr_s, pr_r, rs_s, rs_r, ag_s, ag_r, og_s, og_r, nb_s, nb_r, halo_sem, back_sem,
    pa_s, pa_r, x_s, x_r, pb_s, pb_r,
):
    f, d = lax.axis_index("feat"), lax.axis_index("dp")
    src, width = face.shape
    targets, hid = nb1.shape[0], w1.shape[1]
    own = og.shape[0]
    halo = srows.shape[1]
    full = targets + halo
    mine = pl.ds(pl.multiple_of(f * own, own), own)
    cols = split(width, 256)

    loads = [
        pltpu.make_async_copy(face_hbm.at[:, pl.ds(at, size)], face.at[:, pl.ds(at, size)], load_sem.at[i])
        for i, (at, size) in enumerate(cols)
    ]
    loads.append(pltpu.make_async_copy(w1_hbm, w1, load_sem.at[len(cols)]))
    late = [
        pltpu.make_async_copy(wout_hbm, wout, load_sem.at[len(cols) + 1]),
        pltpu.make_async_copy(win_hbm, win, load_sem.at[len(cols) + 2]),
    ]
    for copy in loads + late:
        copy.start()

    barrier = pltpu.get_barrier_semaphore()
    for i in range(1, n):
        pl.semaphore_signal(barrier, inc=1, device_id={"feat": lax.rem(f + i, n)}, device_id_type=MESH)
    for i in range(1, parts):
        pl.semaphore_signal(barrier, inc=1, device_id={"dp": lax.rem(d + i, parts)}, device_id_type=MESH)

    nb_send[...] = jnp.full(nb_send.shape, -1.0, F32)
    nb_send[:, :own] = live(nb2_t[...], count2[...])
    if nb_all.shape[0] > n * 8:
        nb_all[n * 8 :, :] = jnp.full((nb_all.shape[0] - n * 8, 128), -1.0, F32)
    nb_all[pl.ds(pl.multiple_of(f * 8, 8), 8), :] = nb_send[...]
    og_all[mine, :] = og[...]
    picks[...] = jnp.where(
        lax.broadcasted_iota(jnp.int32, (targets, halo), 0) == srows[...], 1.0, 0.0
    ).astype(BF16)
    names = live(nb1_t[...], count1[...])
    for at in range(0, targets, 128):
        tile = jnp.concatenate([names[:, at : at + 128], jnp.zeros((120, 128), F32)], axis=0)
        nb1[at : at + 128, :] = jnp.transpose(tile)

    blocks = targets // block
    per = block // own
    first = lax.rem(f // per + 1, blocks)
    square = (256, 256)
    eye[...] = jnp.where(
        lax.broadcasted_iota(jnp.int32, square, 0) == lax.broadcasted_iota(jnp.int32, square, 1), 1.0, 0.0
    ).astype(BF16)
    counts_matrix(nb1, pl.multiple_of(first * block, block), adj, 0, block, src)

    pl.semaphore_wait(barrier, n - 1 + parts - 1)

    pair = f + 1 - 2 * lax.rem(f, 2)
    outer = n // 2

    def held(buffer, owner):
        return buffer.at[pl.ds(pl.multiple_of(owner * own, own), own)]

    def gather(source, buffer, sends, recvs):
        first_hop = [
            pltpu.make_async_remote_copy(
                source, held(buffer, f), sends.at[0, i], recvs.at[0, i],
                device_id={"feat": lax.rem(f + 2 * i, n)}, device_id_type=MESH,
            )
            for i in range(1, outer)
        ]
        to_mate = [
            pltpu.make_async_remote_copy(
                source, held(buffer, f), sends.at[1, 0], recvs.at[1, 0],
                device_id={"feat": pair}, device_id_type=MESH,
            )
        ]
        for copy in first_hop + to_mate:
            copy.start()

        def onward():
            for i in range(1, outer):
                first_hop[i - 1].wait_recv()
                owner = held(buffer, lax.rem(f + n - 2 * i, n))
                copy = pltpu.make_async_remote_copy(
                    owner, owner, sends.at[1, i], recvs.at[1, i],
                    device_id={"feat": pair}, device_id_type=MESH,
                )
                copy.start()
                to_mate.append(copy)

        def finish():
            for copy in first_hop:
                copy.wait_send()
            for copy in to_mate:
                copy.wait()

        return onward, finish

    nb_copies = []
    for i in range(1, n):
        copy = pltpu.make_async_remote_copy(
            nb_send, nb_all.at[pl.ds(pl.multiple_of(f * 8, 8), 8)], nb_s.at[i], nb_r.at[i],
            device_id={"feat": lax.rem(f + i, n)}, device_id_type=MESH,
        )
        copy.start()
        nb_copies.append(copy)
    og_onward, og_finish = gather(og, og_all, og_s, og_r)

    column, parity = f // 2, lax.rem(f, 2)

    def to_pair(other):
        there = pl.ds(pl.multiple_of((2 * other + 1 - parity) * own, own), own)
        return pltpu.make_async_remote_copy(
            part16.at[there], pair_buf.at[other], pr_s.at[other], pr_r.at[other],
            device_id={"feat": pair}, device_id_type=MESH,
        )

    def to_owner(other):
        return pltpu.make_async_remote_copy(
            sums.at[other], rs_buf.at[column], rs_s.at[other], rs_r.at[column],
            device_id={"feat": 2 * other + parity}, device_id_type=MESH,
        )

    def by_columns(fn, first_col, last_col):
        if width % 256 == 0:
            pl.loop(first_col, last_col)(lambda j: fn(pl.multiple_of(j * 256, 256), 256))
        else:
            for lane, size in cols[first_col:last_col]:
                fn(lane, size)

    for copy in loads:
        copy.wait()

    def first_layer(i):
        which = lax.rem(first + i, blocks)
        at = pl.multiple_of(which * block, block)
        rows = pl.ds(at, block)
        if blocks > 1:
            pl.when(i > 0)(lambda: counts_matrix(nb1, at, adj, 0, block, src))
        inv = inverse(nb1[rows, :8])
        part32[rows, :] = jnp.zeros((block, hid), F32)

        def column_part(lane, size):
            chunk = pl.ds(lane, size)
            value = dot(adj[...], face[:, chunk]) * inv + face[rows, chunk].astype(F32)
            value = value.astype(BF16)
            agg[rows, chunk] = value
            part32[rows, :] += dot(value, w1[chunk, :])

        by_columns(column_part, 0, len(cols))
        part16[rows, :] = part32[rows, :].astype(BF16)
        for j in range(per // 2):
            to_pair(which * (per // 2) + j).start()

    steps(blocks, first_layer)

    side_size = outer // 2
    side_at = column // side_size * side_size
    far_at = (outer - side_size) - side_at
    far = [far_at + lax.rem(column + i, side_size) for i in range(side_size)]
    near = [side_at + lax.rem(column + i, side_size) for i in range(1, side_size)]

    def pair_sum(other):
        to_pair(other).wait_recv()
        rows = pl.ds(pl.multiple_of((2 * other + parity) * own, own), own)
        return part32[rows, :] + pair_buf[other].astype(F32)

    for other in far + near:
        sums[other] = pair_sum(other).astype(BF16)
        to_owner(other).start()
    pre_sum[...] = pair_sum(column) + b1[...]
    og_onward()

    for copy in nb_copies:
        copy.wait()
    for at in range(0, nb_all.shape[0], 128):
        turned = jnp.transpose(nb_all[at : at + 128, :])
        for j in range(min(16, n - at // 8)):
            t = at // 8 + j
            nb_nat[t * own : (t + 1) * own, :8] = turned[:own, j * 8 : j * 8 + 8]
    counts_matrix(nb_nat, 0, smat, 0, targets, full)
    picks_t[...] = jnp.transpose(picks[...])

    def turn_smat(j):
        lane = pl.ds(pl.multiple_of(j * 128, 128), 128)
        smat_t[lane, :] = dot_last(eye[:128, :128], smat[:, lane]).astype(BF16)

    pl.loop(0, full // 128)(turn_smat)

    value = pre_sum[...]
    for other in far + near:
        pltpu.make_async_remote_copy(
            sums.at[other], rs_buf.at[other], rs_s.at[other], rs_r.at[other],
            device_id={"feat": 2 * other + parity}, device_id_type=MESH,
        ).wait_recv()
        value = value + rs_buf[other].astype(F32)
    pre_own[...] = value.astype(BF16)
    pre_all[mine, :] = value.astype(BF16)
    onward, finish = gather(pre_own, pre_all, ag_s, ag_r)
    for copy in late:
        copy.wait()
    og_finish()

    def out_part(i):
        rows = pl.ds(pl.multiple_of(i * block, block), block)
        grad_act[rows if blocks <= 2 else slice(None), :] = dot_last(og_all[rows, :], wout[...])

    if blocks <= 2:
        steps(blocks, out_part)

    onward()
    early = (len(cols) + 1) // 2

    def turn_agg(lane, size):
        agg_t[pl.ds(lane, size), :] = dot_last(eye[:size, :size], agg[:, pl.ds(lane, size)]).astype(BF16)

    by_columns(turn_agg, 0, early)
    finish()

    def hidden_part(i):
        rows = pl.ds(pl.multiple_of(i * block, block), block)
        value = pre_all[rows, :].astype(F32)
        ext[rows, :] = (value * sigmoid(value)).astype(BF16)

    steps(blocks, hidden_part)
    halo_out[...] = dot(picks_t[...], ext[:targets, :]).astype(BF16)
    halo_copy = pltpu.make_async_remote_copy(
        halo_out, ext.at[pl.ds(targets, halo)], halo_sem.at[0], halo_sem.at[1],
        device_id={"dp": lax.rem(d + 1, parts)}, device_id_type=MESH,
    )
    halo_copy.start()

    def neighbour_part(i):
        rows = pl.ds(pl.multiple_of(i * block, block), block)
        gagg[rows, :] = dot(smat[rows, :targets], ext[:targets, :])

    steps(blocks, neighbour_part)
    by_columns(turn_agg, early, len(cols))
    halo_copy.wait()

    def second_layer(i):
        rows = pl.ds(pl.multiple_of(i * block, block), block)
        inv = inverse(nb_nat[rows, :8])
        if blocks > 2:
            out_part(i)
        total = gagg[rows, :] + dot(smat[rows, targets:], ext[targets:, :])
        value = (ext[rows, :].astype(F32) + total * inv).astype(BF16)
        agg2[rows, :] = value
        step = (grad_act[rows if blocks <= 2 else slice(None), :] * slope(dot(value, win[...]))).astype(BF16)
        back = dot_last(step, win[...])
        gagg[rows, :] = back
        gscaled[rows, :] = (back * inv).astype(BF16)

    steps(blocks, second_layer)

    back_out[...] = dot(smat_t[targets:, :], gscaled[...]).astype(BF16)
    back_copy = pltpu.make_async_remote_copy(
        back_out, back_in, back_sem.at[0], back_sem.at[1],
        device_id={"dp": lax.rem(d + parts - 1, parts)}, device_id_type=MESH,
    )
    back_copy.start()

    for at, size in split(targets, 512):
        rows = slice(at, at + size)
        gtotal[rows, :] = (
            og_all[rows, :].astype(F32) + gagg[rows, :] + dot(smat_t[rows, :], gscaled[...])
        )
    value = dot(agg2[mine, :], win[...])
    act = (value * sigmoid(value)).astype(BF16)
    embed[...] = (ext[mine, :].astype(F32) + dot(act, wout[...])).astype(BF16)

    back_copy.wait()

    def first_gradient(i):
        rows = pl.ds(pl.multiple_of(i * block, block), block)
        value = gtotal[rows, :] + dot(picks[rows, :], back_in[...])
        gp[rows, :] = (value * slope(pre_all[rows, :].astype(F32))).astype(BF16)

    steps(blocks, first_gradient)

    half = width // 2
    size = half // chunks
    side = lax.rem(d, 2)
    chip = d // 2
    chips = parts // 2
    mate = d + 1 - 2 * side

    def place(which, c):
        return pl.ds(pl.multiple_of(which * half + c * size, 16), size)

    pair_copies, chip_copies, end_copies = [], [], []
    for c in range(chunks):
        span = slice(c * size, (c + 1) * size)
        pair_out[span, :] = dot(agg_t[place(1 - side, c), :], gp[...]).astype(BF16)
        copy = pltpu.make_async_remote_copy(
            pair_out.at[pl.ds(c * size, size)], pair_in.at[pl.ds(c * size, size)], pa_s.at[c], pa_r.at[c],
            device_id={"dp": mate}, device_id_type=MESH,
        )
        copy.start()
        pair_copies.append(copy)
    for c in range(chunks):
        span = slice(c * size, (c + 1) * size)
        value = dot(agg_t[place(side, c), :], gp[...])
        pair_copies[c].wait()
        chip_buf[chip, span, :] = (value + pair_in[span, :].astype(F32)).astype(BF16)
        for i in range(1, chips):
            here = chip_buf.at[chip, pl.ds(c * size, size)]
            copy = pltpu.make_async_remote_copy(
                here, here, x_s.at[i, c], x_r.at[i, c],
                device_id={"dp": lax.rem(d + 2 * i, parts)}, device_id_type=MESH,
            )
            copy.start()
            chip_copies.append(copy)
    for c in range(chunks):
        span = slice(c * size, (c + 1) * size)
        for copy in chip_copies[c * (chips - 1) : (c + 1) * (chips - 1)]:
            copy.wait()
        total = chip_buf[0, span, :].astype(F32)
        for i in range(1, chips):
            total = total + chip_buf[i, span, :].astype(F32)
        grad[place(side, c), :] = total.astype(BF16)
        there = grad.at[place(side, c)]
        copy = pltpu.make_async_remote_copy(
            there, there, pb_s.at[c], pb_r.at[c], device_id={"dp": mate}, device_id_type=MESH,
        )
        copy.start()
        end_copies.append(copy)
    for copy in end_copies:
        copy.wait()
    for other in range(outer):
        to_pair(other).wait_send()
    for other in far + near:
        to_owner(other).wait_send()


def finish_kernel(embed_in, grad_in, embed, grad, narrow, wide, in_sem, out_sem):
    rows, pieces = grad_in.shape[0], in_sem.shape[0] - 1
    size = rows // pieces
    small = pltpu.make_async_copy(embed_in, embed, in_sem.at[pieces])
    small.start()

    def part(ref, i):
        return ref.at[pl.ds(i * size, size)]

    arrive = [
        pltpu.make_async_copy(part(grad_in, i), part(narrow, i), in_sem.at[i]) for i in range(pieces)
    ]
    leave = [pltpu.make_async_copy(part(wide, i), part(grad, i), out_sem.at[i]) for i in range(pieces)]
    for copy in arrive:
        copy.start()
    for i in range(pieces):
        arrive[i].wait()
        span = slice(i * size, (i + 1) * size)
        wide[span, :] = narrow[span, :].astype(F32)
        leave[i].start()
    small.wait()
    for copy in leave:
        copy.wait()


def finished(embed, grad):
    pieces = next(c for c in (4, 2, 1) if (grad.shape[0] // c) % 16 == 0)
    any_space = pl.BlockSpec(memory_space=pl.ANY)
    return pl.pallas_call(
        finish_kernel,
        out_shape=(
            jax.ShapeDtypeStruct(embed.shape, BF16),
            jax.ShapeDtypeStruct(grad.shape, F32),
        ),
        in_specs=[any_space, any_space],
        out_specs=(any_space, any_space),
        scratch_shapes=[
            pltpu.VMEM(grad.shape, BF16),
            pltpu.VMEM(grad.shape, F32),
            pltpu.SemaphoreType.DMA((pieces + 1,)),
            pltpu.SemaphoreType.DMA((pieces,)),
        ],
        compiler_params=pltpu.CompilerParams(vmem_limit_bytes=56 * 1024 * 1024),
        name="finish",
    )(embed, grad)


def fused(
    n, parts, face_grid, nb1, count1, w_first, b_first, send_rows, nb2, count2, w_in, w_out, out_grad
):
    src, width = face_grid.shape
    targets, hid = nb1.shape[1], w_first.shape[1]
    inner = w_in.shape[1]
    own, halo = nb2.shape[1], send_rows.shape[1]
    full = targets + halo
    block = min(targets, 256)
    half = width // 2
    chunks = next(c for c in (4, 2, 1) if (half // c) % 16 == 0)
    chips = parts // 2
    tiles = -(-n * 8 // 128) * 128
    any_space = pl.BlockSpec(memory_space=pl.ANY)
    vmem = pl.BlockSpec(memory_space=pltpu.VMEM)
    dma = pltpu.SemaphoreType.DMA
    return pl.pallas_call(
        functools.partial(kernel, n, parts, block, chunks),
        out_shape=(
            jax.ShapeDtypeStruct((own, hid), BF16),
            jax.ShapeDtypeStruct((width, hid), BF16),
        ),
        in_specs=[
            any_space, vmem, vmem, any_space, vmem, vmem, vmem, vmem, any_space, any_space, vmem,
        ],
        out_specs=(vmem, vmem),
        scratch_shapes=[
            pltpu.VMEM((src, width), BF16),
            pltpu.VMEM((width, hid), BF16),
            pltpu.VMEM((hid, inner), BF16),
            pltpu.VMEM((inner, hid), BF16),
            pltpu.VMEM((block, src), BF16),
            pltpu.VMEM((targets, width), BF16),
            pltpu.VMEM((width, targets), BF16),
            pltpu.VMEM((targets, hid), F32),
            pltpu.VMEM((targets, hid), BF16),
            pltpu.VMEM((n // 2, own, hid), BF16),
            pltpu.VMEM((n // 2, own, hid), BF16),
            pltpu.VMEM((own, hid), F32),
            pltpu.VMEM((n // 2, own, hid), BF16),
            pltpu.VMEM((own, hid), BF16),
            pltpu.VMEM((targets, hid), BF16),
            pltpu.VMEM((full, hid), BF16),
            pltpu.VMEM((targets, halo), BF16),
            pltpu.VMEM((halo, targets), BF16),
            pltpu.VMEM((targets, hid), BF16),
            pltpu.VMEM((targets, 128), F32),
            pltpu.VMEM((8, 128), F32),
            pltpu.VMEM((tiles, 128), F32),
            pltpu.VMEM((targets, 128), F32),
            pltpu.VMEM((targets, full), BF16),
            pltpu.VMEM((full, targets), BF16),
            pltpu.VMEM((targets if targets // block <= 2 else block, inner), F32),
            pltpu.VMEM((targets, hid), BF16),
            pltpu.VMEM((targets, hid), BF16),
            pltpu.VMEM((targets, hid), F32),
            pltpu.VMEM((halo, hid), BF16),
            pltpu.VMEM((halo, hid), BF16),
            pltpu.VMEM((halo, hid), BF16),
            pltpu.VMEM((targets, hid), F32),
            pltpu.VMEM((targets, hid), BF16),
            pltpu.VMEM((half, hid), BF16),
            pltpu.VMEM((half, hid), BF16),
            pltpu.VMEM((chips, half, hid), BF16),
            pltpu.VMEM((256, 256), BF16),
            dma((len(split(width, 256)) + 3,)),
            dma((n // 2,)), dma((n // 2,)), dma((n // 2,)), dma((n // 2,)),
            dma((2, n // 2)), dma((2, n // 2)), dma((2, n // 2)), dma((2, n // 2)),
            dma((n,)), dma((n,)),
            dma((2,)), dma((2,)),
            dma((chunks,)), dma((chunks,)),
            dma((chips, chunks)), dma((chips, chunks)),
            dma((chunks,)), dma((chunks,)),
        ],
        compiler_params=pltpu.CompilerParams(
            collective_id=0, has_side_effects=True, vmem_limit_bytes=60 * 1024 * 1024
        ),
        cost_estimate=pl.CostEstimate(
            flops=2 * targets * src * width, bytes_accessed=2 * src * width, transcendentals=0
        ),
        name="fused_step",
    )(
        face_grid, nb1, count1, w_first, b_first, send_rows, nb2, count2, w_in, w_out, out_grad
    )


def solution(mesh):
    n, parts = mesh.shape["feat"], mesh.shape["dp"]

    def body(
        face_grid, first_nbrs, first_count, w_first, b_first, send_rows,
        second_nbrs, second_count, w_in, w_out, out_grad,
    ):
        embed, grad = fused(
            n, parts, face_grid, first_nbrs.T, first_count.reshape(1, -1), w_first,
            b_first.reshape(1, -1), send_rows.reshape(1, -1), second_nbrs.T,
            second_count.reshape(1, -1), w_in, w_out, out_grad,
        )
        return finished(embed, grad)

    return jax.shard_map(
        body,
        mesh=mesh,
        in_specs=(
            P("dp", "feat"), P("dp", None), P("dp"), P("feat", None), P(), P("dp"),
            P(("dp", "feat"), None), P(("dp", "feat")), P(), P(), P(("dp", "feat"), None),
        ),
        out_specs=(P(("dp", "feat"), None), P("feat", None)),
        check_vma=False,
    )
```

```python
import functools

import jax
import jax.numpy as jnp
from jax import lax
from jax.experimental import pallas as pl
from jax.experimental.pallas import tpu as pltpu
from jax.sharding import PartitionSpec as P

MESH = pl.DeviceIdType.MESH
F32, BF16 = jnp.float32, jnp.bfloat16


def dot(a, b):
    return jnp.dot(a, b, preferred_element_type=F32)


def dot_last(a, b):
    return lax.dot_general(a, b, (((1,), (1,)), ((), ())), preferred_element_type=F32)


def sigmoid(value):
    return 0.5 * jnp.tanh(0.5 * value) + 0.5


def slope(value):
    sig = sigmoid(value)
    return sig * (1.0 + value * (1.0 - sig))


def steps(count, fn):
    if count <= 1:
        for i in range(count):
            fn(i)
    else:
        pl.loop(0, count)(fn)


def split(size, width):
    return [(at, min(width, size - at)) for at in range(0, size, width)]


def counts_matrix(nbrs, source, out, at, rows, width):
    spots = [
        (lane, size, (lax.broadcasted_iota(jnp.int32, (8, size), 1) + lane).astype(F32))
        for lane, size in split(width, 1024)
    ]

    def group(g):
        for lane, size, spot in spots:
            pieces = []
            for piece in range(2):
                names = nbrs[pl.ds(pl.multiple_of(source + g * 16 + piece * 8, 8), 8), :8]
                total = jnp.zeros((8, size), F32)
                for slot in range(8):
                    total = total + jnp.where(names[:, slot : slot + 1] == spot, 1.0, 0.0)
                pieces.append(total)
            here = pl.ds(pl.multiple_of(at + g * 16, 16), 16)
            out[here, lane : lane + size] = jnp.concatenate(pieces, axis=0).astype(BF16)

    several = 4 if width <= 1024 and rows % 64 == 0 else 1

    def groups(i):
        for j in range(several):
            group(i * several + j)

    pl.loop(0, rows // 16 // several)(groups)


def live(nbrs, count):
    slots = lax.broadcasted_iota(jnp.int32, nbrs.shape, 0)
    return jnp.where(slots < count, nbrs, -1).astype(F32)


def inverse(names):
    live = jnp.where(names >= 0, 1.0, 0.0)
    return 1.0 / jnp.sum(live, axis=1, keepdims=True)


def kernel(
    n, parts, block, chunks,
    face_hbm, nb1_t, count1, w1_hbm, b1, srows, nb2_t, count2, win_hbm, wout_hbm, og,
    embed, grad,
    face, w1, win, wout, adj, agg, agg_t, part32, part16, pair_buf, sums, pre_sum, rs_buf, pre_own, pre_all,
    ext, picks, picks_t, og_all, nb1, nb_send, nb_all, nb_nat, smat, smat_t, grad_act, agg2, gscaled, gagg,
    halo_out, back_out, back_in, gtotal, gp, pair_out, pair_in, chip_buf, eye,
    load_sem, pr_s, pr_r, rs_s, rs_r, ag_s, ag_r, og_s, og_r, nb_s, nb_r, halo_sem, back_sem,
    pa_s, pa_r, x_s, x_r, pb_s, pb_r,
):
    f, d = lax.axis_index("feat"), lax.axis_index("dp")
    src, width = face.shape
    targets, hid = nb1.shape[0], w1.shape[1]
    own = og.shape[0]
    halo = srows.shape[1]
    full = targets + halo
    mine = pl.ds(pl.multiple_of(f * own, own), own)
    cols = split(width, 256)

    loads = [
        pltpu.make_async_copy(face_hbm.at[:, pl.ds(at, size)], face.at[:, pl.ds(at, size)], load_sem.at[i])
        for i, (at, size) in enumerate(cols)
    ]
    loads.append(pltpu.make_async_copy(w1_hbm, w1, load_sem.at[len(cols)]))
    late = [
        pltpu.make_async_copy(wout_hbm, wout, load_sem.at[len(cols) + 1]),
        pltpu.make_async_copy(win_hbm, win, load_sem.at[len(cols) + 2]),
    ]
    for copy in loads + late:
        copy.start()

    barrier = pltpu.get_barrier_semaphore()
    for i in range(1, n):
        pl.semaphore_signal(barrier, inc=1, device_id={"feat": lax.rem(f + i, n)}, device_id_type=MESH)
    for i in range(1, parts):
        pl.semaphore_signal(barrier, inc=1, device_id={"dp": lax.rem(d + i, parts)}, device_id_type=MESH)

    nb_send[...] = jnp.full(nb_send.shape, -1.0, F32)
    nb_send[:, :own] = live(nb2_t[...], count2[...])
    if nb_all.shape[0] > n * 8:
        nb_all[n * 8 :, :] = jnp.full((nb_all.shape[0] - n * 8, 128), -1.0, F32)
    nb_all[pl.ds(pl.multiple_of(f * 8, 8), 8), :] = nb_send[...]
    og_all[mine, :] = og[...]
    picks[...] = jnp.where(
        lax.broadcasted_iota(jnp.int32, (targets, halo), 0) == srows[...], 1.0, 0.0
    ).astype(BF16)
    names = live(nb1_t[...], count1[...])
    for at in range(0, targets, 128):
        tile = jnp.concatenate([names[:, at : at + 128], jnp.zeros((120, 128), F32)], axis=0)
        nb1[at : at + 128, :] = jnp.transpose(tile)

    blocks = targets // block
    per = block // own
    first = lax.rem(f // per + 1, blocks)
    square = (256, 256)
    eye[...] = jnp.where(
        lax.broadcasted_iota(jnp.int32, square, 0) == lax.broadcasted_iota(jnp.int32, square, 1), 1.0, 0.0
    ).astype(BF16)
    counts_matrix(nb1, pl.multiple_of(first * block, block), adj, 0, block, src)

    pl.semaphore_wait(barrier, n - 1 + parts - 1)

    pair = f + 1 - 2 * lax.rem(f, 2)
    outer = n // 2

    def held(buffer, owner):
        return buffer.at[pl.ds(pl.multiple_of(owner * own, own), own)]

    def gather(source, buffer, sends, recvs):
        first_hop = [
            pltpu.make_async_remote_copy(
                source, held(buffer, f), sends.at[0, i], recvs.at[0, i],
                device_id={"feat": lax.rem(f + 2 * i, n)}, device_id_type=MESH,
            )
            for i in range(1, outer)
        ]
        to_mate = [
            pltpu.make_async_remote_copy(
                source, held(buffer, f), sends.at[1, 0], recvs.at[1, 0],
                device_id={"feat": pair}, device_id_type=MESH,
            )
        ]
        for copy in first_hop + to_mate:
            copy.start()

        def onward():
            for i in range(1, outer):
                first_hop[i - 1].wait_recv()
                owner = held(buffer, lax.rem(f + n - 2 * i, n))
                copy = pltpu.make_async_remote_copy(
                    owner, owner, sends.at[1, i], recvs.at[1, i],
                    device_id={"feat": pair}, device_id_type=MESH,
                )
                copy.start()
                to_mate.append(copy)

        def finish():
            for copy in first_hop:
                copy.wait_send()
            for copy in to_mate:
                copy.wait()

        return onward, finish

    nb_copies = []
    for i in range(1, n):
        copy = pltpu.make_async_remote_copy(
            nb_send, nb_all.at[pl.ds(pl.multiple_of(f * 8, 8), 8)], nb_s.at[i], nb_r.at[i],
            device_id={"feat": lax.rem(f + i, n)}, device_id_type=MESH,
        )
        copy.start()
        nb_copies.append(copy)
    og_onward, og_finish = gather(og, og_all, og_s, og_r)

    column, parity = f // 2, lax.rem(f, 2)

    def to_pair(other):
        there = pl.ds(pl.multiple_of((2 * other + 1 - parity) * own, own), own)
        return pltpu.make_async_remote_copy(
            part16.at[there], pair_buf.at[other], pr_s.at[other], pr_r.at[other],
            device_id={"feat": pair}, device_id_type=MESH,
        )

    def to_owner(other):
        return pltpu.make_async_remote_copy(
            sums.at[other], rs_buf.at[column], rs_s.at[other], rs_r.at[column],
            device_id={"feat": 2 * other + parity}, device_id_type=MESH,
        )

    def by_columns(fn, first_col, last_col):
        if width % 256 == 0:
            pl.loop(first_col, last_col)(lambda j: fn(pl.multiple_of(j * 256, 256), 256))
        else:
            for lane, size in cols[first_col:last_col]:
                fn(lane, size)

    for copy in loads:
        copy.wait()

    def first_layer(i):
        which = lax.rem(first + i, blocks)
        at = pl.multiple_of(which * block, block)
        rows = pl.ds(at, block)
        if blocks > 1:
            pl.when(i > 0)(lambda: counts_matrix(nb1, at, adj, 0, block, src))
        inv = inverse(nb1[rows, :8])
        part32[rows, :] = jnp.zeros((block, hid), F32)

        def column_part(lane, size):
            chunk = pl.ds(lane, size)
            value = dot(adj[...], face[:, chunk]) * inv + face[rows, chunk].astype(F32)
            value = value.astype(BF16)
            agg[rows, chunk] = value
            part32[rows, :] += dot(value, w1[chunk, :])

        by_columns(column_part, 0, len(cols))
        part16[rows, :] = part32[rows, :].astype(BF16)
        for j in range(per // 2):
            to_pair(which * (per // 2) + j).start()

    steps(blocks, first_layer)

    side_size = outer // 2
    side_at = column // side_size * side_size
    far_at = (outer - side_size) - side_at
    far = [far_at + lax.rem(column + i, side_size) for i in range(side_size)]
    near = [side_at + lax.rem(column + i, side_size) for i in range(1, side_size)]

    def pair_sum(other):
        to_pair(other).wait_recv()
        rows = pl.ds(pl.multiple_of((2 * other + parity) * own, own), own)
        return part32[rows, :] + pair_buf[other].astype(F32)

    for other in far + near:
        sums[other] = pair_sum(other).astype(BF16)
        to_owner(other).start()
    pre_sum[...] = pair_sum(column) + b1[...]

    for copy in nb_copies:
        copy.wait()
    for at in range(0, nb_all.shape[0], 128):
        turned = jnp.transpose(nb_all[at : at + 128, :])
        for j in range(min(16, n - at // 8)):
            t = at // 8 + j
            nb_nat[t * own : (t + 1) * own, :8] = turned[:own, j * 8 : j * 8 + 8]
    counts_matrix(nb_nat, 0, smat, 0, targets, full)
    picks_t[...] = jnp.transpose(picks[...])

    def turn_smat(j):
        lane = pl.ds(pl.multiple_of(j * 128, 128), 128)
        smat_t[lane, :] = dot_last(eye[:128, :128], smat[:, lane]).astype(BF16)

    og_onward()
    pl.loop(0, full // 128)(turn_smat)

    value = pre_sum[...]
    for other in far + near:
        pltpu.make_async_remote_copy(
            sums.at[other], rs_buf.at[other], rs_s.at[other], rs_r.at[other],
            device_id={"feat": 2 * other + parity}, device_id_type=MESH,
        ).wait_recv()
        value = value + rs_buf[other].astype(F32)
    pre_own[...] = value.astype(BF16)
    pre_all[mine, :] = value.astype(BF16)
    onward, finish = gather(pre_own, pre_all, ag_s, ag_r)

    early = (len(cols) + 1) // 2

    def turn_agg(lane, size):
        agg_t[pl.ds(lane, size), :] = dot_last(eye[:size, :size], agg[:, pl.ds(lane, size)]).astype(BF16)

    by_columns(turn_agg, 0, early)
    onward()
    for copy in late:
        copy.wait()
    og_finish()

    def out_part(i):
        rows = pl.ds(pl.multiple_of(i * block, block), block)
        grad_act[rows if blocks <= 2 else slice(None), :] = dot_last(og_all[rows, :], wout[...])

    if blocks <= 2:
        steps(blocks, out_part)
    finish()

    def hidden_part(i):
        rows = pl.ds(pl.multiple_of(i * block, block), block)
        value = pre_all[rows, :].astype(F32)
        ext[rows, :] = (value * sigmoid(value)).astype(BF16)

    steps(blocks, hidden_part)
    halo_out[...] = dot(picks_t[...], ext[:targets, :]).astype(BF16)
    halo_copy = pltpu.make_async_remote_copy(
        halo_out, ext.at[pl.ds(targets, halo)], halo_sem.at[0], halo_sem.at[1],
        device_id={"dp": lax.rem(d + 1, parts)}, device_id_type=MESH,
    )
    halo_copy.start()

    def neighbour_part(i):
        rows = pl.ds(pl.multiple_of(i * block, block), block)
        gagg[rows, :] = dot(smat[rows, :targets], ext[:targets, :])

    steps(blocks, neighbour_part)
    by_columns(turn_agg, early, len(cols))
    halo_copy.wait()

    def second_layer(i):
        rows = pl.ds(pl.multiple_of(i * block, block), block)
        inv = inverse(nb_nat[rows, :8])
        if blocks > 2:
            out_part(i)
        total = gagg[rows, :] + dot(smat[rows, targets:], ext[targets:, :])
        value = (ext[rows, :].astype(F32) + total * inv).astype(BF16)
        agg2[rows, :] = value
        step = (grad_act[rows if blocks <= 2 else slice(None), :] * slope(dot(value, win[...]))).astype(BF16)
        back = dot_last(step, win[...])
        gagg[rows, :] = back
        gscaled[rows, :] = (back * inv).astype(BF16)

    steps(blocks, second_layer)

    back_out[...] = dot(smat_t[targets:, :], gscaled[...]).astype(BF16)
    back_copy = pltpu.make_async_remote_copy(
        back_out, back_in, back_sem.at[0], back_sem.at[1],
        device_id={"dp": lax.rem(d + parts - 1, parts)}, device_id_type=MESH,
    )
    back_copy.start()

    for at, size in split(targets, 512):
        rows = slice(at, at + size)
        gtotal[rows, :] = (
            og_all[rows, :].astype(F32) + gagg[rows, :] + dot(smat_t[rows, :], gscaled[...])
        )
    value = dot(agg2[mine, :], win[...])
    act = (value * sigmoid(value)).astype(BF16)
    embed[...] = (ext[mine, :].astype(F32) + dot(act, wout[...])).astype(BF16)

    back_copy.wait()

    def first_gradient(i):
        rows = pl.ds(pl.multiple_of(i * block, block), block)
        value = gtotal[rows, :] + dot(picks[rows, :], back_in[...])
        gp[rows, :] = (value * slope(pre_all[rows, :].astype(F32))).astype(BF16)

    steps(blocks, first_gradient)

    half = width // 2
    size = half // chunks
    side = lax.rem(d, 2)
    chip = d // 2
    chips = parts // 2
    mate = d + 1 - 2 * side

    def place(which, c):
        return pl.ds(pl.multiple_of(which * half + c * size, 16), size)

    pair_copies, chip_copies, end_copies = [], [], []
    for c in range(chunks):
        span = slice(c * size, (c + 1) * size)
        pair_out[span, :] = dot(agg_t[place(1 - side, c), :], gp[...]).astype(BF16)
        copy = pltpu.make_async_remote_copy(
            pair_out.at[pl.ds(c * size, size)], pair_in.at[pl.ds(c * size, size)], pa_s.at[c], pa_r.at[c],
            device_id={"dp": mate}, device_id_type=MESH,
        )
        copy.start()
        pair_copies.append(copy)
    for c in range(chunks):
        span = slice(c * size, (c + 1) * size)
        value = dot(agg_t[place(side, c), :], gp[...])
        pair_copies[c].wait()
        chip_buf[chip, span, :] = (value + pair_in[span, :].astype(F32)).astype(BF16)
        for i in range(1, chips):
            here = chip_buf.at[chip, pl.ds(c * size, size)]
            copy = pltpu.make_async_remote_copy(
                here, here, x_s.at[i, c], x_r.at[i, c],
                device_id={"dp": lax.rem(d + 2 * i, parts)}, device_id_type=MESH,
            )
            copy.start()
            chip_copies.append(copy)
    for c in range(chunks):
        span = slice(c * size, (c + 1) * size)
        for copy in chip_copies[c * (chips - 1) : (c + 1) * (chips - 1)]:
            copy.wait()
        total = chip_buf[0, span, :].astype(F32)
        for i in range(1, chips):
            total = total + chip_buf[i, span, :].astype(F32)
        grad[place(side, c), :] = total.astype(BF16)
        there = grad.at[place(side, c)]
        copy = pltpu.make_async_remote_copy(
            there, there, pb_s.at[c], pb_r.at[c], device_id={"dp": mate}, device_id_type=MESH,
        )
        copy.start()
        end_copies.append(copy)
    for copy in end_copies:
        copy.wait()
    for other in range(outer):
        to_pair(other).wait_send()
    for other in far + near:
        to_owner(other).wait_send()


def finish_kernel(embed_in, grad_in, embed, grad, narrow, wide, in_sem, out_sem):
    rows, pieces = grad_in.shape[0], in_sem.shape[0] - 1
    size = rows // pieces
    small = pltpu.make_async_copy(embed_in, embed, in_sem.at[pieces])
    small.start()

    def part(ref, i):
        return ref.at[pl.ds(i * size, size)]

    arrive = [
        pltpu.make_async_copy(part(grad_in, i), part(narrow, i), in_sem.at[i]) for i in range(pieces)
    ]
    leave = [pltpu.make_async_copy(part(wide, i), part(grad, i), out_sem.at[i]) for i in range(pieces)]
    for copy in arrive:
        copy.start()
    for i in range(pieces):
        arrive[i].wait()
        span = slice(i * size, (i + 1) * size)
        wide[span, :] = narrow[span, :].astype(F32)
        leave[i].start()
    small.wait()
    for copy in leave:
        copy.wait()


def finished(embed, grad):
    pieces = next(c for c in (4, 2, 1) if (grad.shape[0] // c) % 16 == 0)
    any_space = pl.BlockSpec(memory_space=pl.ANY)
    return pl.pallas_call(
        finish_kernel,
        out_shape=(
            jax.ShapeDtypeStruct(embed.shape, BF16),
            jax.ShapeDtypeStruct(grad.shape, F32),
        ),
        in_specs=[any_space, any_space],
        out_specs=(any_space, any_space),
        scratch_shapes=[
            pltpu.VMEM(grad.shape, BF16),
            pltpu.VMEM(grad.shape, F32),
            pltpu.SemaphoreType.DMA((pieces + 1,)),
            pltpu.SemaphoreType.DMA((pieces,)),
        ],
        compiler_params=pltpu.CompilerParams(vmem_limit_bytes=56 * 1024 * 1024),
        name="finish",
    )(embed, grad)


def fused(
    n, parts, face_grid, nb1, count1, w_first, b_first, send_rows, nb2, count2, w_in, w_out, out_grad
):
    src, width = face_grid.shape
    targets, hid = nb1.shape[1], w_first.shape[1]
    inner = w_in.shape[1]
    own, halo = nb2.shape[1], send_rows.shape[1]
    full = targets + halo
    block = min(targets, 256)
    half = width // 2
    chunks = next(c for c in (4, 2, 1) if (half // c) % 16 == 0)
    chips = parts // 2
    tiles = -(-n * 8 // 128) * 128
    any_space = pl.BlockSpec(memory_space=pl.ANY)
    vmem = pl.BlockSpec(memory_space=pltpu.VMEM)
    dma = pltpu.SemaphoreType.DMA
    return pl.pallas_call(
        functools.partial(kernel, n, parts, block, chunks),
        out_shape=(
            jax.ShapeDtypeStruct((own, hid), BF16),
            jax.ShapeDtypeStruct((width, hid), BF16),
        ),
        in_specs=[
            any_space, vmem, vmem, any_space, vmem, vmem, vmem, vmem, any_space, any_space, vmem,
        ],
        out_specs=(vmem, vmem),
        scratch_shapes=[
            pltpu.VMEM((src, width), BF16),
            pltpu.VMEM((width, hid), BF16),
            pltpu.VMEM((hid, inner), BF16),
            pltpu.VMEM((inner, hid), BF16),
            pltpu.VMEM((block, src), BF16),
            pltpu.VMEM((targets, width), BF16),
            pltpu.VMEM((width, targets), BF16),
            pltpu.VMEM((targets, hid), F32),
            pltpu.VMEM((targets, hid), BF16),
            pltpu.VMEM((n // 2, own, hid), BF16),
            pltpu.VMEM((n // 2, own, hid), BF16),
            pltpu.VMEM((own, hid), F32),
            pltpu.VMEM((n // 2, own, hid), BF16),
            pltpu.VMEM((own, hid), BF16),
            pltpu.VMEM((targets, hid), BF16),
            pltpu.VMEM((full, hid), BF16),
            pltpu.VMEM((targets, halo), BF16),
            pltpu.VMEM((halo, targets), BF16),
            pltpu.VMEM((targets, hid), BF16),
            pltpu.VMEM((targets, 128), F32),
            pltpu.VMEM((8, 128), F32),
            pltpu.VMEM((tiles, 128), F32),
            pltpu.VMEM((targets, 128), F32),
            pltpu.VMEM((targets, full), BF16),
            pltpu.VMEM((full, targets), BF16),
            pltpu.VMEM((targets if targets // block <= 2 else block, inner), F32),
            pltpu.VMEM((targets, hid), BF16),
            pltpu.VMEM((targets, hid), BF16),
            pltpu.VMEM((targets, hid), F32),
            pltpu.VMEM((halo, hid), BF16),
            pltpu.VMEM((halo, hid), BF16),
            pltpu.VMEM((halo, hid), BF16),
            pltpu.VMEM((targets, hid), F32),
            pltpu.VMEM((targets, hid), BF16),
            pltpu.VMEM((half, hid), BF16),
            pltpu.VMEM((half, hid), BF16),
            pltpu.VMEM((chips, half, hid), BF16),
            pltpu.VMEM((256, 256), BF16),
            dma((len(split(width, 256)) + 3,)),
            dma((n // 2,)), dma((n // 2,)), dma((n // 2,)), dma((n // 2,)),
            dma((2, n // 2)), dma((2, n // 2)), dma((2, n // 2)), dma((2, n // 2)),
            dma((n,)), dma((n,)),
            dma((2,)), dma((2,)),
            dma((chunks,)), dma((chunks,)),
            dma((chips, chunks)), dma((chips, chunks)),
            dma((chunks,)), dma((chunks,)),
        ],
        compiler_params=pltpu.CompilerParams(
            collective_id=0, has_side_effects=True, vmem_limit_bytes=60 * 1024 * 1024
        ),
        cost_estimate=pl.CostEstimate(
            flops=2 * targets * src * width, bytes_accessed=2 * src * width, transcendentals=0
        ),
        name="fused_step",
    )(
        face_grid, nb1, count1, w_first, b_first, send_rows, nb2, count2, w_in, w_out, out_grad
    )


def solution(mesh):
    n, parts = mesh.shape["feat"], mesh.shape["dp"]

    def body(
        face_grid, first_nbrs, first_count, w_first, b_first, send_rows,
        second_nbrs, second_count, w_in, w_out, out_grad,
    ):
        embed, grad = fused(
            n, parts, face_grid, first_nbrs.T, first_count.reshape(1, -1), w_first,
            b_first.reshape(1, -1), send_rows.reshape(1, -1), second_nbrs.T,
            second_count.reshape(1, -1), w_in, w_out, out_grad,
        )
        return finished(embed, grad)

    return jax.shard_map(
        body,
        mesh=mesh,
        in_specs=(
            P("dp", "feat"), P("dp", None), P("dp"), P("feat", None), P(), P("dp"),
            P(("dp", "feat"), None), P(("dp", "feat")), P(), P(), P(("dp", "feat"), None),
        ),
        out_specs=(P(("dp", "feat"), None), P("feat", None)),
        check_vma=False,
    )
```
